128 devices in a mesh: dp: 8 (over x_lo, z), tensor: 16 (over x_hi, y, core).
Axes of the slice: x: 4 (x_hi: 2, x_lo: 2; x = x_hi * 2 + x_lo), y: 4, z: 4, core: 2. Of those that a mesh axis runs over, the one named last changes fastest.
Arguments:
- inputs: bfloat16 [4, 512, 8192], P(None, 'dp'), may hold values from -6 to 6
- norm_gain: float32 [8192], replicated, may hold values from 0.5 to 1.5
- w_query: bfloat16 [8192, 4096], P(None, 'tensor'), may hold values from -0.0625 to 0.0625
- w_kv: bfloat16 [8192, 4096], P(None, 'tensor'), may hold values from -1 to 1, as said below
- w_out: bfloat16 [4096, 8192], P('tensor'), may hold values from -0.09375 to 0.09375
- kv_cache: bfloat16 [512, 16, 256, 256], P('dp', 'tensor'), may hold values from -420 to 420, as said below
- kv_lengths: int32 [512], P('dp'), may hold values from 1 to 256, 81920 in all
- reuse_dist: int32 [8], replicated, may hold values from 1 to 64, as said below
- shard_map: int32 [16], replicated, may hold values from 0 to 15, each once
- holder_weights: bfloat16 [8, 8192, 4096], P(None, ('dp', 'tensor')), may hold values from -0.29882812 to 0.29882812
Outputs:
- outputs: bfloat16 [4, 512, 8192], P(None, 'dp')
- next_weights: bfloat16 [8192, 4096], P(None, 'tensor')
The draws below stay inside these ranges and needn't reach their ends.
Inputs may be any that keep to these rules, and one draw needn't show every extreme that they name: `w_kv`: columns of ranks t and u are equal when t // 4 == u // 4. `kv_cache`: blocks of ranks t and u are equal when t // 4 == u // 4. `reuse_dist`: the distances are distinct.
All inputs are finite; a program needn't handle non-finite values. No bound on the sum of `kv_lengths` on one device may be relied on, other than what follows from the above.
Results may differ from the reference program's by a relative error of at most 0.011.
Values may be sent and summed in bfloat16 or wider, within the bound.
A program may use at most 128 MiB of HBM per device.

```python
import math
import jax
import jax.numpy as jnp
import numpy as np
from jax import lax

D = 8192
HD = 128
SHARE = 4
STEPS = 4
CAND = 8
CTX = 256
RANKS = 16
QCOLS = 4096
ROWS = 512


def draw_w_kv(key, part):
    key = jax.random.fold_in(key, 5)
    base = jnp.clip(jax.random.normal(key, (D, RANKS // SHARE, 2 * HD), jnp.float32), -5.0, 5.0) * (1.0 / D ** 0.5)
    whole = jnp.repeat(base, SHARE, axis=1).reshape(D, RANKS * 2 * HD)
    return whole.astype(jnp.bfloat16)


def draw_kv_cache(key, part):
    key = jax.random.fold_in(key, 7)
    first = jax.random.fold_in(key, 0)
    groups = RANKS // SHARE
    base = jnp.clip(jax.random.normal(first, (ROWS, groups, CTX, 2 * HD), jnp.float32), -5.0, 5.0)
    whole = jnp.repeat(base, SHARE, axis=1)
    return whole.astype(jnp.bfloat16)


def draw_reuse_dist(key, part):
    key = jax.random.fold_in(key, 11)
    first, second = jax.random.split(key, 2)
    middle = jax.random.permutation(first, 62)[:CAND - 2] + 2
    ends = jnp.array([1, 64], dtype=jnp.int32)
    values = jnp.concatenate([ends, middle.astype(jnp.int32)])
    return jax.random.permutation(second, values).astype(jnp.int32)


def shard_levels(key, extent, cuts, low, largest):
    level, own = 1.0, jax.random.fold_in(key, 6)
    for dim, blocks in cuts:
        draws = jnp.exp(jax.random.uniform(jax.random.fold_in(own, dim), (blocks,), jnp.float32, low / len(cuts), largest / len(cuts)))
        level = level * jnp.repeat(draws, extent[dim] // blocks).reshape([-1 if axis == dim else 1 for axis in range(len(extent))])
    return level


def profile(number_of, total, bound, skew):
    portions = [(1 << 20) // math.isqrt(grade ** skew) + 1 for grade in range(2, number_of + 1)]
    surplus, holding = total - bound - (number_of - 1), [1] * (number_of - 1)
    while surplus > 0:
        candidates = [i for i in range(number_of - 1) if holding[i] < bound]
        mass, remaining = sum([portions[i] for i in candidates]), surplus
        for i in candidates:
            more = min(bound - holding[i], max(1, remaining * portions[i] // mass), surplus)
            holding[i] = holding[i] + more
            surplus = surplus - more
    return np.array([bound] + holding)


def ragged_sizes(rng, amount, total, reach, slope):
    if amount == 2:
        one = jax.random.randint(rng, (), max(1, total - reach), min(reach, total - 1) + 1)
        return jnp.stack([one, total - one])
    lengths = jnp.asarray(profile(amount, total, reach, slope), jnp.int32)
    twos = (amount - 1) // 2
    source_of, receiver = lengths[1:1 + 2 * twos:2], lengths[2:2 + 2 * twos:2]
    margin = jnp.minimum(source_of - 1, reach - receiver)
    shifted = jax.random.randint(jax.random.fold_in(rng, 1), (twos,), 0, 1 << 20) % (margin + 1)
    lengths = lengths.at[1:1 + 2 * twos:2].set(source_of - shifted).at[2:2 + 2 * twos:2].set(receiver + shifted)
    return lengths[jax.random.permutation(jax.random.fold_in(rng, 2), amount)]


def normal_values(rng, shape, scale, bound, shards=(), kind=jnp.bfloat16):
    factor_of = shard_levels(rng, shape, shards, -0.22, 0.18) if shards else 1.0
    values = jax.random.normal(rng, shape, jnp.float32) * scale * factor_of
    return jnp.minimum(jnp.maximum(values, -bound), bound).astype(kind)


def setup_inputs(seed: int = 0) -> dict:
    seeds = jax.random.split(jax.random.key(seed), 11)
    return {
        "inputs": normal_values(seeds[0], (STEPS, ROWS, D), 1.0, 6.0, ((1, 8),)),
        "norm_gain": jnp.clip(1.0 + 0.1 * jax.random.normal(seeds[1], (D,), jnp.float32), 0.5, 1.5),
        "w_query": normal_values(seeds[2], (D, QCOLS), D ** -0.5, 0.0625, ((1, 16),)),
        "w_kv": draw_w_kv(jax.random.fold_in(seeds[10], 71), 0),
        "w_out": normal_values(seeds[4], (QCOLS, D), QCOLS ** -0.5, 0.09375, ((0, 16),)),
        "kv_cache": draw_kv_cache(jax.random.fold_in(seeds[10], 71), 0),
        "kv_lengths": ragged_sizes(seeds[6], ROWS, ROWS * CTX * 5 // 8, CTX, 1).astype(jnp.int32),
        "reuse_dist": draw_reuse_dist(jax.random.fold_in(seeds[10], 71), 0),
        "shard_map": jax.random.permutation(seeds[8], RANKS).astype(jnp.int32),
        "holder_weights": normal_values(seeds[9], (CAND, D, QCOLS), 0.05, 0.29882812, ((1, 128),)),
    }


def rotate(vec, pos):
    half = vec.shape[-1] // 2
    expo = jnp.arange(half, dtype=jnp.float32) * (2.0 / vec.shape[-1])
    inverse = jnp.float32(1000000.0) ** (-expo)
    angle = pos[:, None] * inverse[None, :]
    cosine = jnp.cos(angle)[:, None, :]
    sine = jnp.sin(angle)[:, None, :]
    low = vec[..., :half]
    high = vec[..., half:]
    return jnp.concatenate([low * cosine - high * sine, high * cosine + low * sine], axis=-1)

def reference(inputs, norm_gain, w_query, w_kv, w_out, kv_cache, kv_lengths, reuse_dist, shard_map, holder_weights):
    ranks = kv_cache.shape[1]
    rows = inputs.shape[1]
    ctx = kv_cache.shape[2]
    heads_dev = w_query.shape[1] // ranks // HD
    scale = 1.0 / math.sqrt(HD)
    valid = jnp.arange(ctx, dtype=jnp.int32)[None, :] < kv_lengths[:, None]
    new_keys = jnp.zeros((rows, ranks, STEPS, HD), jnp.bfloat16)
    new_vals = jnp.zeros((rows, ranks, STEPS, HD), jnp.bfloat16)
    results = []
    for step in range(STEPS):
        xs = inputs[step].astype(jnp.float32)
        normed = (xs * lax.rsqrt(lax.optimization_barrier(jnp.mean(xs * xs, axis=-1, keepdims=True)) + 1e-06) * norm_gain).astype(jnp.bfloat16)
        query = jnp.dot(normed, w_query, preferred_element_type=jnp.float32).reshape(rows, ranks * heads_dev, HD)
        pair = jnp.dot(normed, w_kv, preferred_element_type=jnp.float32).reshape(rows, ranks, 2 * HD)
        pos = (kv_lengths + step).astype(jnp.float32)
        query = rotate(query, pos).astype(jnp.bfloat16)
        key_now = rotate(pair[..., :HD], pos).astype(jnp.bfloat16)
        new_keys = new_keys.at[:, :, step].set(key_now)
        new_vals = new_vals.at[:, :, step].set(pair[..., HD:].astype(jnp.bfloat16))
        fresh_mask = jnp.arange(STEPS) <= step
        pieces = []
        for rank in range(ranks):
            qt = query[:, rank * heads_dev:(rank + 1) * heads_dev].astype(jnp.float32)
            ckeys = kv_cache[:, rank, :, :HD].astype(jnp.float32)
            cvals = kv_cache[:, rank, :, HD:].astype(jnp.float32)
            cache_scores = jnp.einsum('rhd,rcd->rhc', qt, ckeys) * scale
            cache_scores = jnp.where(valid[:, None, :], cache_scores, -jnp.inf)
            fresh_scores = jnp.einsum('rhd,rjd->rhj', qt, new_keys[:, rank].astype(jnp.float32)) * scale
            fresh_scores = jnp.where(fresh_mask[None, None, :], fresh_scores, -jnp.inf)
            top = jnp.maximum(lax.optimization_barrier(jnp.max(cache_scores, axis=-1)), lax.optimization_barrier(jnp.max(fresh_scores, axis=-1)))[..., None]
            cache_exp = jnp.exp(cache_scores - top)
            fresh_exp = jnp.exp(fresh_scores - top)
            total = lax.optimization_barrier(jnp.sum(cache_exp, axis=-1, keepdims=True)) + lax.optimization_barrier(jnp.sum(fresh_exp, axis=-1, keepdims=True))
            cache_w = (cache_exp / total).astype(jnp.bfloat16).astype(jnp.float32)
            fresh_w = (fresh_exp / total).astype(jnp.bfloat16).astype(jnp.float32)
            mixed = jnp.einsum('rhc,rcd->rhd', cache_w, cvals) + jnp.einsum('rhj,rjd->rhd', fresh_w, new_vals[:, rank].astype(jnp.float32))
            pieces.append(mixed.astype(jnp.bfloat16))
        attended = jnp.concatenate(pieces, axis=1).reshape(rows, ranks * heads_dev * HD)
        projected = jnp.dot(attended, w_out, preferred_element_type=jnp.float32)
        results.append((xs + projected).astype(jnp.bfloat16))
    outputs = jnp.stack(results)
    chosen = jnp.argmin(reuse_dist).astype(jnp.int32)
    picked = lax.dynamic_index_in_dim(holder_weights, chosen, 0, keepdims=False)
    width = picked.shape[1] // ranks
    blocks = picked.reshape(picked.shape[0], ranks, width)
    next_weights = jnp.take(blocks, shard_map, axis=1).reshape(picked.shape[0], ranks * width)
    return (outputs, next_weights)
```

```python
import functools
import math

import jax
import jax.numpy as jnp
import numpy as np
from jax import lax
from jax.experimental import pallas as pl
from jax.experimental.pallas import tpu as pltpu
from jax.sharding import PartitionSpec as P

MESH = pl.DeviceIdType.MESH
HD = 128
STEPS = 4
ROWS = 64
HALF = 32
WIDTH = 8192
CHUNK = 1024
NCHUNK = WIDTH // CHUNK
COLS = 4096
CTX = 256
NCOPY = 96
BF = jnp.bfloat16
F32 = jnp.float32


def mult(value, by):
    return pl.multiple_of(value, by)


def kernel(
    x_hbm, gain, wq_hbm, wkv_hbm, wo_hbm, kv_hbm, len_v, dist, smap, hold_hbm, inverse,
    out, nw,
    xv, w, wo, kv, hold, ordr, w1r, acc, sq, ybf, cs, sn, qs, qr, kn, vn, qf, sc, fs, pw, pf, mix,
    att, part, ra, rax, rbx, rb, sa, sb, keep_a, keep_b,
    ld, chunk_sem, hold_sem, ssem, rsem,
):
    dp = lax.axis_index("dp")
    tensor = lax.axis_index("tensor")
    xl, z = dp // 4, lax.rem(dp, 4)
    xh, y, c = tensor // 8, lax.rem(tensor // 2, 4), lax.rem(tensor, 2)

    def dev(xl_, xh_, y_, z_, c_):
        return (xl_ * 4 + z_, xh_ * 8 + y_ * 2 + c_)

    def ring(value, by):
        return lax.rem(value + by + 4, 4)

    copies = []

    def send(src, dst, where):
        i = len(copies)
        cp = pltpu.make_async_remote_copy(
            src_ref=src, dst_ref=dst, send_sem=ssem.at[i], recv_sem=rsem.at[i],
            device_id=where, device_id_type=MESH,
        )
        cp.start()
        copies.append([cp, False])
        return i

    def arrived(i):
        copies[i][0].wait_recv()
        copies[i][1] = True

    sibling = dev(xl, xh, y, z, 1 - c)
    across = dev(xl, 1 - xh, y, z, c)
    cross = dev(1 - xl, 1 - xh, y, z, c)
    near = dev(1 - xl, xh, y, z, c)
    z_up = dev(xl, xh, y, ring(z, 1), c)
    z_down = dev(xl, xh, y, ring(z, -1), c)

    def same_core(k):
        return dev(xl, xh, ring(y, k), z, c)

    def hold_load(t):
        cols = pl.ds(mult(t * 256, 256), 256)
        return pltpu.make_async_copy(hold_hbm.at[:, :, cols], hold.at[:, t], hold_sem.at[t])

    def start_hold(t, carry):
        hold_load(t).start()
        return carry

    lax.fori_loop(0, 16, start_hold, 0)

    def chunk_loads(i):
        ks = pl.ds(mult(i * CHUNK, CHUNK), CHUNK)
        return (
            pltpu.make_async_copy(x_hbm.at[:, :, ks], xv.at[:, :, ks], chunk_sem.at[i, 0]),
            pltpu.make_async_copy(wq_hbm.at[ks], w.at[ks, pl.ds(0, 256)], chunk_sem.at[i, 1]),
            pltpu.make_async_copy(wkv_hbm.at[ks], w.at[ks, pl.ds(256, 256)], chunk_sem.at[i, 2]),
        )

    def start_chunk(i, carry):
        for cp in chunk_loads(i):
            cp.start()
        return carry

    lax.fori_loop(0, NCHUNK, start_chunk, 0)
    my_half = pl.ds(mult(c * HALF, HALF), HALF)
    load_kv = pltpu.make_async_copy(kv_hbm.at[my_half, 0], kv, ld.at[1])
    load_kv.start()
    my_cols = pl.ds(mult(c * COLS, COLS), COLS)
    sib_cols = pl.ds(mult((1 - c) * COLS, COLS), COLS)
    my_wo = pl.ds(mult(c * 256, 256), 256)
    load_wo = pltpu.make_async_copy(wo_hbm.at[:, my_cols], wo.at[my_wo], ld.at[2])
    load_wo.start()

    barrier = pltpu.get_barrier_semaphore()
    greet = [sibling, across, cross, near, z_up, z_down]
    for k in (1, 2, 3):
        for other in (c, 1 - c):
            greet.append(dev(xl, xh, ring(y, k), z, other))
    for where in greet:
        pl.semaphore_signal(barrier, inc=1, device_id=where, device_id_type=MESH)

    lengths = len_v[...].astype(F32)
    eye = lax.broadcasted_iota(jnp.int32, (ROWS, ROWS), 0) == lax.broadcasted_iota(
        jnp.int32, (ROWS, ROWS), 1
    )
    position = jnp.sum(jnp.where(eye, lengths, 0.0), axis=1, keepdims=True)
    sign = jnp.where(lax.broadcasted_iota(jnp.int32, (1, HD), 1) < HD // 2, -1.0, 1.0)
    for s in range(STEPS):
        angle = (position + float(s)) * inverse[...]
        cs[s] = jnp.cos(angle)
        sn[s] = jnp.sin(angle) * sign
    acc[...] = jnp.zeros_like(acc)
    sq[...] = jnp.zeros_like(sq)

    best = dist[0] * 8
    for i in range(1, 8):
        best = jnp.minimum(best, dist[i] * 8 + i)
    chosen = lax.rem(best, 8)

    def hold_done(t, carry):
        hold_load(t).wait()
        return carry

    def order(t, carry):
        ordr[t] = hold[chosen, smap[t]]
        return carry

    lax.fori_loop(0, 16, hold_done, 0)
    lax.fori_loop(0, 16, order, 0)

    pl.semaphore_wait(barrier, len(greet))

    def rows_of(xl_, xh_, y_, z_, c_):
        return pl.ds(mult(((xl_ * 4 + z_) * 16 + xh_ * 8 + y_ * 2 + c_) * 64, 64), 64)

    def slab_of(xl_, xh_, z_):
        return pl.ds(mult(((xl_ * 4 + z_) * 16 + xh_ * 8) * 64, 512), 512)

    cross_copy = send(ordr.at[pl.ds(mult((1 - xh) * 8, 8), 8)], w1r, cross)
    mine = rows_of(xl, xh, y, z, c)
    own_copies = []
    for k in (2, 1, 3, 0):
        for flip in (0, 1):
            if k == 0 and flip == 0:
                continue
            yk = ring(y, k)
            ck = (c, 1 - c)[flip]
            own_copies.append(
                send(ordr.at[xh * 8 + yk * 2 + ck], nw.at[mine], dev(xl, xh, yk, z, ck))
            )
    nw[mine] = ordr[xh * 8 + y * 2 + c]
    wo_copy = send(wo_hbm.at[:, sib_cols], wo.at[my_wo], sibling)

    def project(i, carry):
        ks = pl.ds(mult(i * CHUNK, CHUNK), CHUNK)
        for cp in chunk_loads(i):
            cp.wait()
        g = gain[:, ks]
        for s in range(STEPS):
            xs = xv[s, :, ks].astype(F32)
            ybf[s] = (xs * g).astype(BF)
            xx = xs * xs
            total = xx[:, 0:128]
            for j in range(1, CHUNK // 128):
                total = total + xx[:, j * 128:(j + 1) * 128]
            sq[s] += total
        acc[...] += jnp.dot(
            ybf[...].reshape(STEPS * ROWS, CHUNK), w[ks, :], preferred_element_type=F32
        )
        return carry

    lax.fori_loop(0, NCHUNK, project, 0)

    def turn(v, s):
        return v * cs[s] + pltpu.roll(v, HD // 2, 1) * sn[s]

    for s in range(STEPS):
        scale = lax.rsqrt(jnp.sum(sq[s], axis=1, keepdims=True) * (1.0 / WIDTH) + 1e-06)
        block = pl.ds(s * ROWS, ROWS)
        for h in range(2):
            cols = slice(h * HD, (h + 1) * HD)
            qs[s, :, cols] = turn(acc[block, cols] * scale, s).astype(BF)
        kn[s] = turn(acc[block, 256:384] * scale, s).astype(BF)
        vn[s] = (acc[block, 384:512] * scale).astype(BF)

    sib_half = pl.ds(mult((1 - c) * HALF, HALF), HALF)
    q_copy = send(qs.at[:, sib_half, :], qr, sibling)

    arrived(cross_copy)
    theirs = rows_of(1 - xl, 1 - xh, y, z, c)
    cross_copies = []
    for k in (2, 1, 3, 0):
        for flip in (0, 1):
            if k == 0 and flip == 0:
                continue
            yk = ring(y, k)
            ck = (c, 1 - c)[flip]
            cross_copies.append(
                send(w1r.at[yk * 2 + ck], nw.at[theirs], dev(xl, xh, yk, z, ck))
            )
    nw[theirs] = w1r[y * 2 + c]

    def around(slab):
        return send(nw.at[slab], nw.at[slab], z_up), send(nw.at[slab], nw.at[slab], z_down)

    for i in own_copies:
        arrived(i)
    slab_0a = slab_of(xl, xh, z)
    z_0a = around(slab_0a)
    near_a = send(nw.at[slab_0a], nw.at[slab_0a], near)

    for s in range(STEPS):
        for h in range(2):
            qf[pl.ds(s * 2 + h, HALF, stride=16), :] = qs[s, my_half, h * HD:(h + 1) * HD].astype(
                F32
            )
    arrived(q_copy)
    for s in range(STEPS):
        for h in range(2):
            qf[pl.ds(8 + s * 2 + h, HALF, stride=16), :] = qr[s, :, h * HD:(h + 1) * HD].astype(F32)
    load_kv.wait()

    def score(r, carry):
        rows = pl.ds(mult(r * 16, 16), 16)
        sc[rows, :] = lax.dot_general(
            qf[rows, :].astype(BF), kv[r, :, 0:HD], (((1,), (1,)), ((), ())),
            preferred_element_type=F32,
        )
        return carry

    lax.fori_loop(0, HALF, score, 0, unroll=4)
    keys = kn[:, my_half, :].reshape(STEPS * HALF, HD)
    fs[...] = lax.dot_general(
        qf[...].astype(BF), keys, (((1,), (1,)), ((), ())), preferred_element_type=F32
    )

    for i in cross_copies:
        arrived(i)
    slab_0b = slab_of(1 - xl, 1 - xh, z)
    z_0b = around(slab_0b)
    near_b = send(nw.at[slab_0b], nw.at[slab_0b], near)

    factor = 1.0 / math.sqrt(HD)
    neg = -jnp.inf

    def soften(b, carry):
        rows = pl.ds(mult(b * 64, 64), 64)
        i = lax.broadcasted_iota(jnp.int32, (64, 1), 0) + b * 64
        r = i >> 4
        step = (i & 7) >> 1
        lane = lax.broadcasted_iota(jnp.int32, (1, ROWS), 1)
        limit = jnp.sum(jnp.where(lane == r + c * HALF, lengths, 0.0), axis=1, keepdims=True)
        place = lax.broadcasted_iota(jnp.int32, (1, CTX), 1).astype(F32)
        cached = jnp.where(place < limit, sc[rows, :] * factor, neg)
        n = lax.broadcasted_iota(jnp.int32, (1, 128), 1)
        usable = ((n & 31) == r) & ((n >> 5) <= step)
        fresh = jnp.where(usable, fs[rows, :] * factor, neg)
        top = jnp.maximum(
            jnp.max(cached, axis=1, keepdims=True), jnp.max(fresh, axis=1, keepdims=True)
        )
        ce = jnp.exp(cached - top)
        fe = jnp.exp(fresh - top)
        total = jnp.sum(ce, axis=1, keepdims=True) + jnp.sum(fe, axis=1, keepdims=True)
        share = 1.0 / total
        pw[rows, :] = (ce * share).astype(BF)
        pf[rows, :] = (fe * share).astype(BF)
        return carry

    lax.fori_loop(0, 8, soften, 0)

    values = vn[:, my_half, :].reshape(STEPS * HALF, HD)
    mix[...] = jnp.dot(pf[...], values, preferred_element_type=F32)

    def weigh(r, carry):
        rows = pl.ds(mult(r * 16, 16), 16)
        mix[rows, :] += jnp.dot(pw[rows, :], kv[r, :, HD:2 * HD], preferred_element_type=F32)
        return carry

    lax.fori_loop(0, HALF, weigh, 0, unroll=4)
    for source in range(2):
        for s in range(STEPS):
            for h in range(2):
                base = (c if source == 0 else 1 - c) * 256 + h * HD
                att[s, my_half, pl.ds(mult(base, HD), HD)] = mix[
                    pl.ds(source * 8 + s * 2 + h, HALF, stride=16), :
                ].astype(BF)
    att_copy = send(att.at[:, my_half, :], att.at[:, my_half, :], sibling)
    load_wo.wait()
    arrived(wo_copy)
    arrived(att_copy)

    first = pl.ds(0, 2)
    second = pl.ds(2, 2)
    a_copies, b_copies = {}, {}
    attended = att[...].reshape(STEPS * ROWS, 2 * 256)
    for k in (2, 1, 3, 0):
        yk = ring(y, k)
        for flip in (1, 0):
            side = (xh, 1 - xh)[flip]
            cols = pl.ds(mult(yk * 1024 + side * 512, 512), 512)
            term = jnp.dot(attended, wo[:, cols], preferred_element_type=F32)
            part[:, :, cols] = term.astype(BF).reshape(STEPS, ROWS, 512)
            if flip == 1:
                b_copies[k] = send(part.at[second, :, cols], rbx.at[k], across)
        if k:
            cols = pl.ds(mult(yk * 1024, 1024), 1024)
            a_copies[k] = send(part.at[first, :, cols], ra.at[k - 1], same_core(k))

    slab_1a = slab_of(1 - xl, xh, z)
    slab_1b = slab_of(xl, 1 - xh, z)
    arrived(near_a)
    z_1a = around(slab_1a)
    arrived(near_b)
    z_1b = around(slab_1b)

    b2 = {}
    for k in (2, 1, 3):
        arrived(b_copies[k])
        cols = pl.ds(mult(ring(y, k) * 1024 + xh * 512, 512), 512)
        sb[k - 1] = (part[second, :, cols].astype(F32) + rbx[k].astype(F32)).astype(BF)
        b2[k] = send(sb.at[k - 1], rb.at[k - 1], same_core(k))
    for k in (1, 2, 3):
        arrived(a_copies[k])

    def own_sum(side):
        cols = pl.ds(mult(y * 1024 + side * 512, 512), 512)
        inner = pl.ds(mult(side * 512, 512), 512)
        total = part[first, :, cols].astype(F32)
        for k in (1, 2, 3):
            total = total + ra[k - 1, :, :, inner].astype(F32)
        return total

    sa[...] = own_sum(1 - xh).astype(BF)
    a2 = send(sa, rax, across)
    keep_a[...] = own_sum(xh)
    here = pl.ds(mult(y * 1024 + xh * 512, 512), 512)
    arrived(b_copies[0])
    keep_b[...] = part[second, :, here].astype(F32) + rbx[0].astype(F32)

    def onward(i, slab, where):
        arrived(i)
        return send(nw.at[slab], nw.at[slab], where)

    onward(z_0a[0], slab_of(xl, xh, ring(z, -1)), z_up)
    onward(z_0b[1], slab_of(1 - xl, 1 - xh, ring(z, 1)), z_down)

    def chunk_at(c_, y_, xh_):
        return pl.ds(mult(c_ * COLS + y_ * 1024 + xh_ * 512, 512), 512)

    def give(part_of, cols, wheres):
        ref = out.at[part_of, :, cols]
        return [send(ref, ref, where) for where in wheres]

    own = chunk_at(c, y, xh)
    spread = [across, same_core(2), same_core(1), same_core(3)]
    for k in (1, 2, 3):
        arrived(b2[k])
    total = xv[second, :, own].astype(F32) + keep_b[...]
    for k in (1, 2, 3):
        total = total + rb[k - 1].astype(F32)
    out[second, :, own] = total.astype(BF)
    gb = give(second, own, spread)
    arrived(a2)
    out[first, :, own] = (xv[first, :, own].astype(F32) + keep_a[...] + rax[...].astype(F32)).astype(
        BF
    )
    ga = give(first, own, spread)
    give(second, own, [sibling])
    give(first, own, [sibling])

    onward(z_1a[0], slab_of(1 - xl, xh, ring(z, -1)), z_up)
    onward(z_1b[1], slab_of(xl, 1 - xh, ring(z, 1)), z_down)

    last = []
    for j, k in ((2, 1), (3, 3), (1, 2)):
        arrived(gb[j])
        cols = chunk_at(c, ring(y, -k), xh)
        last.append((second, chunk_at(c, ring(y, -k), 1 - xh), give(second, cols, [across])[0]))
        give(second, cols, [sibling])
    arrived(ga[0])
    cols = chunk_at(c, y, 1 - xh)
    for k, i in zip((2, 1, 3), give(first, cols, spread[1:])):
        last.append((first, chunk_at(c, ring(y, -k), 1 - xh), i))
    give(first, cols, [sibling])
    arrived(gb[0])
    give(second, cols, [sibling])
    for j, k in ((2, 1), (3, 3), (1, 2)):
        arrived(ga[j])
        give(first, chunk_at(c, ring(y, -k), xh), [sibling])
    for part_of, cols, i in last:
        arrived(i)
        give(part_of, cols, [sibling])

    for cp, done in copies:
        if not done:
            cp.wait_recv()
        cp.wait_send()


def on_device(
    inputs, norm_gain, w_query, w_kv, w_out, kv_cache, kv_lengths, reuse_dist, shard_map,
    holder_weights,
):
    expo = np.arange(HD // 2, dtype=np.float32) * np.float32(2.0 / HD)
    inverse = np.float32(1000000.0) ** (-expo)
    inverse = jnp.asarray(np.concatenate([inverse, inverse])[None, :], F32)
    hbm = pl.BlockSpec(memory_space=pltpu.HBM)
    vmem = pl.BlockSpec(memory_space=pltpu.VMEM)
    smem = pl.BlockSpec(memory_space=pltpu.SMEM)
    dma = pltpu.SemaphoreType.DMA
    return pl.pallas_call(
        kernel,
        out_shape=(
            pltpu.VMEM((STEPS, ROWS, WIDTH), BF),
            pltpu.VMEM((WIDTH, 256), BF),
        ),
        in_specs=[hbm, vmem, hbm, hbm, hbm, hbm, vmem, smem, smem, hbm, vmem],
        out_specs=(vmem, vmem),
        scratch_shapes=[
            pltpu.VMEM((STEPS, ROWS, WIDTH), BF),
            pltpu.VMEM((WIDTH, 512), BF),
            pltpu.VMEM((512, COLS), BF),
            pltpu.VMEM((HALF, CTX, 2 * HD), BF),
            pltpu.VMEM((8, 16, 64, 256), BF),
            pltpu.VMEM((16, 64, 256), BF),
            pltpu.VMEM((8, 64, 256), BF),
            pltpu.VMEM((STEPS * ROWS, 512), F32),
            pltpu.VMEM((STEPS, ROWS, 128), F32),
            pltpu.VMEM((STEPS, ROWS, CHUNK), BF),
            pltpu.VMEM((STEPS, ROWS, HD), F32),
            pltpu.VMEM((STEPS, ROWS, HD), F32),
            pltpu.VMEM((STEPS, ROWS, 256), BF),
            pltpu.VMEM((STEPS, HALF, 256), BF),
            pltpu.VMEM((STEPS, ROWS, HD), BF),
            pltpu.VMEM((STEPS, ROWS, HD), BF),
            pltpu.VMEM((512, HD), F32),
            pltpu.VMEM((512, CTX), F32),
            pltpu.VMEM((512, 128), F32),
            pltpu.VMEM((512, CTX), BF),
            pltpu.VMEM((512, 128), BF),
            pltpu.VMEM((512, HD), F32),
            pltpu.VMEM((STEPS, ROWS, 512), BF),
            pltpu.VMEM((STEPS, ROWS, COLS), BF),
            pltpu.VMEM((3, 2, ROWS, 1024), BF),
            pltpu.VMEM((2, ROWS, 512), BF),
            pltpu.VMEM((4, 2, ROWS, 512), BF),
            pltpu.VMEM((3, 2, ROWS, 512), BF),
            pltpu.VMEM((2, ROWS, 512), BF),
            pltpu.VMEM((3, 2, ROWS, 512), BF),
            pltpu.VMEM((2, ROWS, 512), F32),
            pltpu.VMEM((2, ROWS, 512), F32),
            dma((3,)),
            dma((NCHUNK, 3)),
            dma((16,)),
            dma((NCOPY,)),
            dma((NCOPY,)),
        ],
        compiler_params=pltpu.CompilerParams(
            collective_id=0, has_side_effects=True, vmem_limit_bytes=48 * 1024 * 1024
        ),
    )(
        inputs, norm_gain.reshape(1, WIDTH), w_query, w_kv, w_out, kv_cache,
        kv_lengths.reshape(1, ROWS), reuse_dist, shard_map, holder_weights, inverse,
    )


def solution(mesh):
    in_specs = (
        P(None, "dp", None),
        P(),
        P(None, "tensor"),
        P(None, "tensor"),
        P("tensor", None),
        P("dp", "tensor", None, None),
        P("dp"),
        P(),
        P(),
        P(None, ("dp", "tensor"), None),
    )
    out_specs = (P(None, "dp", None), P(None, "tensor"))
    return jax.shard_map(
        on_device, mesh=mesh, in_specs=in_specs, out_specs=out_specs, check_vma=False
    )
```

```python
import functools
import math

import jax
import jax.numpy as jnp
from jax import lax
from jax.experimental import pallas as pl
from jax.experimental.pallas import tpu as pltpu
from jax.sharding import PartitionSpec as P

MESH = pl.DeviceIdType.MESH
HD = 128
STEPS = 4
ROWS = 64
HALF = 32
WIDTH = 8192
CHUNK = 1024
NCHUNK = WIDTH // CHUNK
COLS = 4096
CTX = 256
NCOPY = 96
BF = jnp.bfloat16
F32 = jnp.float32


def mult(value, by):
    return pl.multiple_of(value, by)


def kernel(
    x_hbm, gain_hbm, wq_hbm, wkv_hbm, wo_hbm, kv_hbm, len_hbm, dist_hbm, smap_hbm, hold_hbm,
    out, nw,
    gain, len_v, dist, smap,
    xv, w, wo, kv, hold, ordr, w1r, acc, sq, ybf, cs, sn, qs, qr, kn, vn, qf, bias, bias_f,
    pw, pf, mix, att, part, rbx, rb, sb, keep_b, rel_up, rel_dn, dir_o, dir_n, sum_o, sum_n,
    s_up, s_dn, sa, rax, keep_a,
    ld, chunk_sem, hold_sem, ssem, rsem,
):
    dp = lax.axis_index("dp")
    tensor = lax.axis_index("tensor")
    xl, z = dp // 4, lax.rem(dp, 4)
    xh, y, c = tensor // 8, lax.rem(tensor // 2, 4), lax.rem(tensor, 2)

    def dev(xl_, xh_, y_, z_, c_):
        return (xl_ * 4 + z_, xh_ * 8 + y_ * 2 + c_)

    def ring(value, by):
        return lax.rem(value + by + 4, 4)

    copies = []

    def send(src, dst, where):
        i = len(copies)
        cp = pltpu.make_async_remote_copy(
            src_ref=src, dst_ref=dst, send_sem=ssem.at[i], recv_sem=rsem.at[i],
            device_id=where, device_id_type=MESH,
        )
        cp.start()
        copies.append([cp, False])
        return i

    def arrived(i):
        copies[i][0].wait_recv()
        copies[i][1] = True

    sibling = dev(xl, xh, y, z, 1 - c)
    across = dev(xl, 1 - xh, y, z, c)
    cross = dev(1 - xl, 1 - xh, y, z, c)
    near = dev(1 - xl, xh, y, z, c)
    z_up = dev(xl, xh, y, ring(z, 1), c)
    z_down = dev(xl, xh, y, ring(z, -1), c)

    def same_core(k):
        return dev(xl, xh, ring(y, k), z, c)

    barrier = pltpu.get_barrier_semaphore()
    greet = [sibling, across, cross, near, z_up, z_down]
    for k in (1, 2, 3):
        for other in (c, 1 - c):
            greet.append(dev(xl, xh, ring(y, k), z, other))
    for where in greet:
        pl.semaphore_signal(barrier, inc=1, device_id=where, device_id_type=MESH)

    small = [
        pltpu.make_async_copy(a, b, ld.at[i])
        for i, (a, b) in enumerate(
            ((len_hbm, len_v), (gain_hbm, gain), (dist_hbm, dist), (smap_hbm, smap))
        )
    ]
    for cp in small:
        cp.start()

    def chunk_loads(i):
        ks = pl.ds(mult(i * CHUNK, CHUNK), CHUNK)
        return (
            pltpu.make_async_copy(
                x_hbm.at[:, :, :, :, ks], xv.at[:, :, :, :, ks], chunk_sem.at[i, 0]
            ),
            pltpu.make_async_copy(wq_hbm.at[ks], w.at[ks, pl.ds(0, 256)], chunk_sem.at[i, 1]),
            pltpu.make_async_copy(wkv_hbm.at[ks], w.at[ks, pl.ds(256, 256)], chunk_sem.at[i, 2]),
        )

    def start_chunk(i, carry):
        for cp in chunk_loads(i):
            cp.start()
        return carry

    def hold_load(t):
        cols = pl.ds(mult(t * 256, 256), 256)
        return pltpu.make_async_copy(hold_hbm.at[:, :, cols], hold.at[:, t], hold_sem.at[t])

    def start_hold(t, carry):
        hold_load(t).start()
        return carry

    lax.fori_loop(0, 2, start_chunk, 0)
    lax.fori_loop(0, 16, start_hold, 0)
    lax.fori_loop(2, NCHUNK, start_chunk, 0)
    my_half = pl.ds(mult(c * HALF, HALF), HALF)
    load_kv = pltpu.make_async_copy(kv_hbm.at[my_half, 0], kv, ld.at[4])
    load_kv.start()
    my_cols = pl.ds(mult(c * COLS, COLS), COLS)
    sib_cols = pl.ds(mult((1 - c) * COLS, COLS), COLS)
    my_wo = pl.ds(mult(c * 256, 256), 256)
    load_wo = pltpu.make_async_copy(wo_hbm.at[:, my_cols], wo.at[my_wo], ld.at[5])
    load_wo.start()

    acc[...] = jnp.zeros_like(acc)
    sq[...] = jnp.zeros_like(sq)
    for cp in small:
        cp.wait()
    lengths = len_v[...].astype(F32)
    eye = lax.broadcasted_iota(jnp.int32, (ROWS, ROWS), 0) == lax.broadcasted_iota(
        jnp.int32, (ROWS, ROWS), 1
    )
    position = jnp.sum(jnp.where(eye, lengths, 0.0), axis=1, keepdims=True)
    lane = lax.broadcasted_iota(jnp.int32, (1, HD), 1)
    sign = jnp.where(lane < HD // 2, -1.0, 1.0)
    inverse = jnp.exp((lane & (HD // 2 - 1)).astype(F32) * (-math.log(1000000.0) / (HD // 2)))
    for s in range(STEPS):
        angle = (position + float(s)) * inverse
        cs[s] = jnp.cos(angle)
        sn[s] = jnp.sin(angle) * sign

    def mask(b, carry):
        rows = pl.ds(mult(b * 128, 128), 128)
        i = lax.broadcasted_iota(jnp.int32, (128, 1), 0) + b * 128
        r = i >> 4
        step = (i & 7) >> 1
        row_lane = lax.broadcasted_iota(jnp.int32, (1, ROWS), 1)
        limit = jnp.sum(jnp.where(row_lane == r + c * HALF, lengths, 0.0), axis=1, keepdims=True)
        place = lax.broadcasted_iota(jnp.int32, (1, CTX), 1).astype(F32)
        bias[rows, :] = jnp.where(place < limit, 0.0, -jnp.inf)
        n = lax.broadcasted_iota(jnp.int32, (1, 64), 1)
        usable = ((n & 15) == (r & 15)) & ((n >> 4) <= step)
        bias_f[rows, :] = jnp.where(usable, 0.0, -jnp.inf)
        return carry

    lax.fori_loop(0, 4, mask, 0)

    def project(i, carry):
        ks = pl.ds(mult(i * CHUNK, CHUNK), CHUNK)
        for cp in chunk_loads(i):
            cp.wait()
        g = gain[:, ks]
        for s in range(STEPS):
            xs = xv[s, :, :, :, ks].reshape(ROWS, CHUNK).astype(F32)
            ybf[s] = (xs * g).astype(BF)
            xx = xs * xs
            total = xx[:, 0:128]
            for j in range(1, CHUNK // 128):
                total = total + xx[:, j * 128:(j + 1) * 128]
            sq[s] += total
        acc[...] += jnp.dot(
            ybf[...].reshape(STEPS * ROWS, CHUNK), w[ks, :], preferred_element_type=F32
        )
        return carry

    lax.fori_loop(0, 2, project, 0)

    best = dist[0] * 8
    for i in range(1, 8):
        best = jnp.minimum(best, dist[i] * 8 + i)
    chosen = lax.rem(best, 8)

    def hold_done(t, carry):
        hold_load(t).wait()
        return carry

    def order(t, carry):
        ordr[t] = hold[chosen, smap[t]]
        return carry

    lax.fori_loop(0, 16, hold_done, 0)
    lax.fori_loop(0, 16, order, 0)

    pl.semaphore_wait(barrier, len(greet))

    def rows_of(xl_, xh_, y_, z_, c_):
        return pl.ds(mult(((xl_ * 4 + z_) * 16 + xh_ * 8 + y_ * 2 + c_) * 64, 64), 64)

    def slab_of(xl_, xh_, z_):
        return pl.ds(mult(((xl_ * 4 + z_) * 16 + xh_ * 8) * 64, 512), 512)

    mine = rows_of(xl, xh, y, z, c)
    own_copies = []
    for k in (2, 1, 3, 0):
        for flip in (0, 1):
            if k == 0 and flip == 0:
                continue
            yk = ring(y, k)
            ck = (c, 1 - c)[flip]
            own_copies.append(
                send(ordr.at[xh * 8 + yk * 2 + ck], nw.at[mine], dev(xl, xh, yk, z, ck))
            )
    cross_copy = send(ordr.at[pl.ds(mult((1 - xh) * 8, 8), 8)], w1r, cross)
    nw[mine] = ordr[xh * 8 + y * 2 + c]
    wo_copy = send(wo_hbm.at[:, sib_cols], wo.at[my_wo], sibling)

    lax.fori_loop(2, NCHUNK, project, 0)

    def turn(v, s):
        return v * cs[s] + pltpu.roll(v, HD // 2, 1) * sn[s]

    for s in range(STEPS):
        scale = lax.rsqrt(jnp.sum(sq[s], axis=1, keepdims=True) * (1.0 / WIDTH) + 1e-06)
        block = pl.ds(s * ROWS, ROWS)
        for h in range(2):
            cols = slice(h * HD, (h + 1) * HD)
            qs[s, :, cols] = turn(acc[block, cols] * scale, s).astype(BF)
        kn[s] = turn(acc[block, 256:384] * scale, s).astype(BF)
        vn[s] = (acc[block, 384:512] * scale).astype(BF)

    sib_half = pl.ds(mult((1 - c) * HALF, HALF), HALF)
    q_copy = send(qs.at[:, sib_half, :], qr, sibling)
    for s in range(STEPS):
        for h in range(2):
            qf[pl.ds(s * 2 + h, HALF, stride=16), :] = qs[s, my_half, h * HD:(h + 1) * HD].astype(
                F32
            )

    def around(slab):
        return send(nw.at[slab], nw.at[slab], z_up), send(nw.at[slab], nw.at[slab], z_down)

    for i in own_copies:
        arrived(i)
    slab_0a = slab_of(xl, xh, z)
    z_0a = around(slab_0a)
    near_a = send(nw.at[slab_0a], nw.at[slab_0a], near)

    arrived(q_copy)
    for s in range(STEPS):
        for h in range(2):
            qf[pl.ds(8 + s * 2 + h, HALF, stride=16), :] = qr[s, :, h * HD:(h + 1) * HD].astype(F32)
    load_kv.wait()

    factor = 1.0 / math.sqrt(HD)

    def attend(b):
        block = pl.ds(b * 256, 256)
        sub = pl.ds(mult(c * HALF + b * 16, 16), 16)

        def score(i, carry):
            rows = pl.ds(mult(b * 256 + i * 16, 16), 16)
            mine_ = pl.ds(mult(i * 16, 16), 16)
            bias_here = bias[rows, :]
            got = lax.dot_general(
                qf[rows, :].astype(BF), kv[b * 16 + i, :, 0:HD], (((1,), (1,)), ((), ())),
                preferred_element_type=F32,
            )
            bias[rows, :] = got * factor + bias_here
            return carry

        lax.fori_loop(0, 16, score, 0, unroll=8)
        keys = kn[:, sub, :].reshape(STEPS * 16, HD)
        for part_of in range(2):
            rows = pl.ds(b * 256 + part_of * 128, 128)
            fresh = lax.dot_general(
                qf[rows, :].astype(BF), keys, (((1,), (1,)), ((), ())), preferred_element_type=F32
            ) * factor + bias_f[rows, :]
            cached = bias[rows, :]
            top = jnp.maximum(
                jnp.max(cached, axis=1, keepdims=True), jnp.max(fresh, axis=1, keepdims=True)
            )
            ce = jnp.exp(cached - top)
            fe = jnp.exp(fresh - top)
            total = jnp.sum(ce, axis=1, keepdims=True) + jnp.sum(fe, axis=1, keepdims=True)
            share = 1.0 / total
            pw[rows, :] = (ce * share).astype(BF)
            pf[rows, :] = (fe * share).astype(BF)
        values = vn[:, sub, :].reshape(STEPS * 16, HD)
        mix[block, :] = jnp.dot(pf[block, :], values, preferred_element_type=F32)

        def weigh(i, carry):
            rows = pl.ds(mult(b * 256 + i * 16, 16), 16)
            mix[rows, :] += jnp.dot(
                pw[rows, :], kv[b * 16 + i, :, HD:2 * HD], preferred_element_type=F32
            )
            return carry

        lax.fori_loop(0, 16, weigh, 0, unroll=8)
        for source in range(2):
            for s in range(STEPS):
                for h in range(2):
                    base = (c if source == 0 else 1 - c) * 256 + h * HD
                    att[b, s, c, :, pl.ds(mult(base, HD), HD)] = mix[
                        pl.ds(b * 256 + source * 8 + s * 2 + h, 16, stride=16), :
                    ].astype(BF)
        return send(att.at[b, :, c], att.at[b, :, c], sibling)

    def block_cols(yk, side):
        return pl.ds(mult(yk * 1024 + side * 512, 512), 512)

    def term(b, yk, side):
        cols = block_cols(yk, side)
        part[b, :, cols] = jnp.dot(
            att[b].reshape(128, 512), wo[:, cols], preferred_element_type=F32
        ).astype(BF)
        return part.at[b, :, cols]

    up, down, far = ring(y, 1), ring(y, -1), ring(y, 2)
    to_up, to_down = same_core(1), same_core(-1)

    att_b = attend(0)

    arrived(cross_copy)
    theirs = rows_of(1 - xl, 1 - xh, y, z, c)
    cross_copies = []
    for k in (2, 1, 3, 0):
        for flip in (0, 1):
            if k == 0 and flip == 0:
                continue
            yk = ring(y, k)
            ck = (c, 1 - c)[flip]
            cross_copies.append(
                send(w1r.at[yk * 2 + ck], nw.at[theirs], dev(xl, xh, yk, z, ck))
            )
    nw[theirs] = w1r[y * 2 + c]

    load_wo.wait()
    arrived(wo_copy)
    arrived(att_b)
    b_copies, b2 = {}, {}
    for k in (2, 1, 3, 0):
        b_copies[k] = send(term(0, ring(y, k), 1 - xh), rbx.at[k], across)
    for k in (2, 1, 3, 0):
        term(0, ring(y, k), xh)

    att_a = attend(1)

    for i in cross_copies:
        arrived(i)
    slab_0b = slab_of(1 - xl, 1 - xh, z)
    z_0b = around(slab_0b)
    near_b = send(nw.at[slab_0b], nw.at[slab_0b], near)

    arrived(att_a)
    r_up = send(term(1, far, 1 - xh), rel_up, to_up)
    r_dn = send(term(1, far, xh), rel_dn, to_down)
    d_dn = send(term(1, down, 1 - xh), dir_o, to_down)
    d_up = send(term(1, up, xh), dir_n, to_up)
    term(1, up, 1 - xh)
    term(1, down, xh)
    term(1, y, 1 - xh)
    term(1, y, xh)

    def pass_on(k):
        arrived(b_copies[k])
        cols = block_cols(ring(y, k), xh)
        sb[k - 1] = (part[0, :, cols].astype(F32) + rbx[k].astype(F32)).astype(BF)
        b2[k] = send(sb.at[k - 1], rb.at[k - 1], same_core(k))

    pass_on(2)
    arrived(near_a)
    slab_1a = slab_of(1 - xl, xh, z)
    slab_1b = slab_of(xl, 1 - xh, z)
    z_1a = around(slab_1a)
    pass_on(1)
    arrived(r_up)
    s_up[...] = (part[1, :, block_cols(up, 1 - xh)].astype(F32) + rel_up[...].astype(F32)).astype(BF)
    t_up = send(s_up, sum_o, to_up)
    arrived(r_dn)
    s_dn[...] = (part[1, :, block_cols(down, xh)].astype(F32) + rel_dn[...].astype(F32)).astype(BF)
    t_dn = send(s_dn, sum_n, to_down)
    pass_on(3)

    def onward(i, slab, where):
        arrived(i)
        return send(nw.at[slab], nw.at[slab], where)

    onward(z_0a[0], slab_of(xl, xh, ring(z, -1)), z_up)
    arrived(near_b)
    z_1b = around(slab_1b)
    arrived(b_copies[0])
    keep_b[...] = part[0, :, block_cols(y, xh)].astype(F32) + rbx[0].astype(F32)
    onward(z_0b[1], slab_of(1 - xl, 1 - xh, ring(z, 1)), z_down)

    arrived(d_dn)
    arrived(t_up)
    sa[...] = (
        part[1, :, block_cols(y, 1 - xh)].astype(F32)
        + dir_o[...].astype(F32)
        + sum_o[...].astype(F32)
    ).astype(BF)
    a2 = send(sa, rax, across)
    arrived(d_up)
    arrived(t_dn)
    keep_a[...] = (
        part[1, :, block_cols(y, xh)].astype(F32)
        + dir_n[...].astype(F32)
        + sum_n[...].astype(F32)
    )

    def chunk_at(c_, y_, xh_, off=0, size=512):
        return pl.ds(mult(c_ * COLS + y_ * 1024 + xh_ * 512 + off, 128), size)

    def give(b, cols, *wheres):
        ref = out.at[:, :, b, :, cols]
        return [send(ref, ref, where) for where in wheres]

    def finish(b, total):
        cols = chunk_at(c, y, xh)
        whole = xv[:, :, b, :, cols].astype(F32) + total.reshape(STEPS, 2, 16, 512)
        out[:, :, b, :, cols] = whole.astype(BF)

    own = chunk_at(c, y, xh)
    other = chunk_at(c, y, 1 - xh)
    for k in (1, 3, 2):
        arrived(b2[k])
    finish(0, keep_b[...] + rb[0].astype(F32) + rb[1].astype(F32) + rb[2].astype(F32))
    gb_far, gb_up, gb_dn, gb_x = give(0, own, same_core(2), to_up, to_down, across)
    give(0, own, sibling)
    arrived(a2)
    finish(1, keep_a[...] + rax[...].astype(F32))
    ga_x, ga_up, ga_dn = give(1, own, across, to_up, to_down)
    give(1, own, sibling)

    onward(z_1a[0], slab_of(1 - xl, xh, ring(z, -1)), z_up)
    onward(z_1b[1], slab_of(xl, 1 - xh, ring(z, 1)), z_down)

    last = []

    def to_across(i, yk):
        arrived(i)
        cols = chunk_at(c, yk, xh)
        (j,) = give(0, cols, across)
        last.append((j, 0, chunk_at(c, yk, 1 - xh)))
        give(0, cols, sibling)

    def relay(i_up, i_dn, side):
        arrived(i_up)
        (first,) = give(1, chunk_at(c, down, side, 0, 256), to_up)
        arrived(i_dn)
        (second,) = give(1, chunk_at(c, up, side, 256, 256), to_down)
        give(1, chunk_at(c, down, side), sibling)
        give(1, chunk_at(c, up, side), sibling)
        return first, second

    to_across(gb_up, down)
    to_across(gb_dn, up)
    to_across(gb_far, far)
    arrived(gb_x)
    give(0, other, sibling)
    arrived(ga_x)
    oa_up, oa_dn = give(1, other, to_up, to_down)
    give(1, other, sibling)
    near_1, near_2 = relay(ga_up, ga_dn, xh)
    far_1, far_2 = relay(oa_up, oa_dn, 1 - xh)
    for i in (near_1, near_2):
        arrived(i)
    give(1, chunk_at(c, far, xh), sibling)
    for i, b, cols in last:
        arrived(i)
        give(b, cols, sibling)
    for i in (far_1, far_2):
        arrived(i)
    give(1, chunk_at(c, far, 1 - xh), sibling)

    for cp, done in copies:
        if not done:
            cp.wait_recv()
        cp.wait_send()


def on_device(
    inputs, norm_gain, w_query, w_kv, w_out, kv_cache, kv_lengths, reuse_dist, shard_map,
    holder_weights,
):
    hbm = pl.BlockSpec(memory_space=pltpu.HBM)
    vmem = pl.BlockSpec(memory_space=pltpu.VMEM)
    dma = pltpu.SemaphoreType.DMA
    block = (128, 512)
    outputs, next_weights = pl.pallas_call(
        kernel,
        out_shape=(
            pltpu.VMEM((STEPS, 2, 2, 16, WIDTH), BF),
            pltpu.VMEM((WIDTH, 256), BF),
        ),
        in_specs=[hbm] * 10,
        out_specs=(vmem, vmem),
        scratch_shapes=[
            pltpu.VMEM((1, WIDTH), F32),
            pltpu.VMEM((1, ROWS), jnp.int32),
            pltpu.SMEM((8,), jnp.int32),
            pltpu.SMEM((16,), jnp.int32),
            pltpu.VMEM((STEPS, 2, 2, 16, WIDTH), BF),
            pltpu.VMEM((WIDTH, 512), BF),
            pltpu.VMEM((512, COLS), BF),
            pltpu.VMEM((HALF, CTX, 2 * HD), BF),
            pltpu.VMEM((8, 16, 64, 256), BF),
            pltpu.VMEM((16, 64, 256), BF),
            pltpu.VMEM((8, 64, 256), BF),
            pltpu.VMEM((STEPS * ROWS, 512), F32),
            pltpu.VMEM((STEPS, ROWS, 128), F32),
            pltpu.VMEM((STEPS, ROWS, CHUNK), BF),
            pltpu.VMEM((STEPS, ROWS, HD), F32),
            pltpu.VMEM((STEPS, ROWS, HD), F32),
            pltpu.VMEM((STEPS, ROWS, 256), BF),
            pltpu.VMEM((STEPS, HALF, 256), BF),
            pltpu.VMEM((STEPS, ROWS, HD), BF),
            pltpu.VMEM((STEPS, ROWS, HD), BF),
            pltpu.VMEM((512, HD), F32),
            pltpu.VMEM((512, CTX), F32),
            pltpu.VMEM((512, 64), F32),
            pltpu.VMEM((512, CTX), BF),
            pltpu.VMEM((512, 64), BF),
            pltpu.VMEM((512, HD), F32),
            pltpu.VMEM((2, STEPS, 2, 16, 512), BF),
            pltpu.VMEM((2, 128, COLS), BF),
            pltpu.VMEM((4,) + block, BF),
            pltpu.VMEM((3,) + block, BF),
            pltpu.VMEM((3,) + block, BF),
            pltpu.VMEM(block, F32),
            pltpu.VMEM(block, BF),
            pltpu.VMEM(block, BF),
            pltpu.VMEM(block, BF),
            pltpu.VMEM(block, BF),
            pltpu.VMEM(block, BF),
            pltpu.VMEM(block, BF),
            pltpu.VMEM(block, BF),
            pltpu.VMEM(block, BF),
            pltpu.VMEM(block, BF),
            pltpu.VMEM(block, BF),
            pltpu.VMEM(block, F32),
            dma((6,)),
            dma((NCHUNK, 3)),
            dma((16,)),
            dma((NCOPY,)),
            dma((NCOPY,)),
        ],
        compiler_params=pltpu.CompilerParams(
            collective_id=0, has_side_effects=True, vmem_limit_bytes=48 * 1024 * 1024
        ),
    )(
        inputs.reshape(STEPS, 2, 2, 16, WIDTH), norm_gain.reshape(1, WIDTH), w_query, w_kv, w_out,
        kv_cache, kv_lengths.reshape(1, ROWS), reuse_dist, shard_map, holder_weights,
    )
    return outputs.reshape(STEPS, ROWS, WIDTH), next_weights


def solution(mesh):
    in_specs = (
        P(None, "dp", None),
        P(),
        P(None, "tensor"),
        P(None, "tensor"),
        P("tensor", None),
        P("dp", "tensor", None, None),
        P("dp"),
        P(),
        P(),
        P(None, ("dp", "tensor"), None),
    )
    out_specs = (P(None, "dp", None), P(None, "tensor"))
    return jax.shard_map(
        on_device, mesh=mesh, in_specs=in_specs, out_specs=out_specs, check_vma=False
    )
```

```python
import functools
import math

import jax
import jax.numpy as jnp
from jax import lax
from jax.experimental import pallas as pl
from jax.experimental.pallas import tpu as pltpu
from jax.sharding import PartitionSpec as P

MESH = pl.DeviceIdType.MESH
HD = 128
STEPS = 4
ROWS = 64
HALF = 32
WIDTH = 8192
CHUNK = 1024
NCHUNK = WIDTH // CHUNK
COLS = 4096
CTX = 256
NCOPY = 84
BF = jnp.bfloat16
F32 = jnp.float32


def mult(value, by):
    return pl.multiple_of(value, by)


def kernel(
    x_hbm, gain_hbm, wq_hbm, wkv_hbm, wo_hbm, kv_hbm, len_hbm, dist_hbm, smap_hbm, hold_hbm,
    out, nw,
    gain, len_v, dist, smap,
    xv, w, wo, kv, hold, ordr, w1r, acc, sq, ybf, cs, sn, qs, qr, kn, vn, qf, bias, bias_f,
    pw, pf, mix, att, part, rbx, rb, sb, keep_b, rel_up, rel_dn, dir_o, dir_n, sum_o, sum_n,
    s_up, s_dn, sa, rax, keep_a,
    ld, chunk_sem, ssem, rsem,
):
    dp = lax.axis_index("dp")
    tensor = lax.axis_index("tensor")
    xl, z = dp // 4, lax.rem(dp, 4)
    xh, y, c = tensor // 8, lax.rem(tensor // 2, 4), lax.rem(tensor, 2)

    def dev(xl_, xh_, y_, z_, c_):
        return (xl_ * 4 + z_, xh_ * 8 + y_ * 2 + c_)

    def ring(value, by):
        return lax.rem(value + by + 4, 4)

    used, sent, pending = [], [0, 0, 0, 0], {}

    def flag():
        used.append(0)
        return len(used) - 1

    def kib(ref):
        return math.prod(ref.shape) * 2 // 1024

    def send(src, dst, where, group=None, lane=0):
        i = flag() if group is None else group
        pltpu.make_async_remote_copy(
            src_ref=src, dst_ref=dst, send_sem=ssem.at[lane], recv_sem=rsem.at[i],
            device_id=where, device_id_type=MESH,
        ).start()
        sent[lane] += kib(src)
        pending[i] = pending.get(i, 0) + kib(dst)
        return i

    def wait_kib(sem, amount):
        ref = w.at[pl.ds(0, amount)]
        pltpu.make_async_copy(ref, ref, sem).wait()

    def arrived(i):
        wait_kib(rsem.at[i], pending.pop(i))

    sibling = dev(xl, xh, y, z, 1 - c)
    across = dev(xl, 1 - xh, y, z, c)
    cross = dev(1 - xl, 1 - xh, y, z, c)
    near = dev(1 - xl, xh, y, z, c)
    z_up = dev(xl, xh, y, ring(z, 1), c)
    z_down = dev(xl, xh, y, ring(z, -1), c)

    def same_core(k):
        return dev(xl, xh, ring(y, k), z, c)

    barrier = pltpu.get_barrier_semaphore()
    greet = [sibling, across, cross, near, z_up, z_down]
    for k in (1, 2, 3):
        for other in (c, 1 - c):
            greet.append(dev(xl, xh, ring(y, k), z, other))
    for where in greet:
        pl.semaphore_signal(barrier, inc=1, device_id=where, device_id_type=MESH)

    small = [
        pltpu.make_async_copy(a, b, ld.at[i])
        for i, (a, b) in enumerate(
            ((len_hbm, len_v), (gain_hbm, gain), (dist_hbm, dist), (smap_hbm, smap))
        )
    ]
    for cp in small:
        cp.start()

    def chunk_loads(i):
        ks = pl.ds(mult(i * CHUNK, CHUNK), CHUNK)
        return (
            pltpu.make_async_copy(
                x_hbm.at[:, :, :, :, ks], xv.at[:, :, :, :, ks], chunk_sem.at[i, 0]
            ),
            pltpu.make_async_copy(wq_hbm.at[ks], w.at[ks, pl.ds(0, 256)], chunk_sem.at[i, 1]),
            pltpu.make_async_copy(wkv_hbm.at[ks], w.at[ks, pl.ds(256, 256)], chunk_sem.at[i, 1]),
        )

    def start_chunk(i, carry):
        for cp in chunk_loads(i):
            cp.start()
        return carry

    def wait_chunk(i):
        ks = pl.ds(mult(i * CHUNK, CHUNK), CHUNK)
        chunk_loads(i)[0].wait()
        pltpu.make_async_copy(w.at[ks], w.at[ks], chunk_sem.at[i, 1]).wait()

    def start_hold(t, carry):
        cols = pl.ds(mult(t * 256, 256), 256)
        pltpu.make_async_copy(hold_hbm.at[:, :, cols], hold.at[:, t], ld.at[6]).start()
        return carry

    lax.fori_loop(0, 2, start_chunk, 0)
    lax.fori_loop(0, 16, start_hold, 0)
    lax.fori_loop(2, NCHUNK, start_chunk, 0)
    my_half = pl.ds(mult(c * HALF, HALF), HALF)
    load_kv = pltpu.make_async_copy(kv_hbm.at[my_half, 0], kv, ld.at[4])
    load_kv.start()
    my_cols = pl.ds(mult(c * COLS, COLS), COLS)
    sib_cols = pl.ds(mult((1 - c) * COLS, COLS), COLS)
    my_wo = pl.ds(mult(c * 256, 256), 256)
    load_wo = pltpu.make_async_copy(wo_hbm.at[:, my_cols], wo.at[my_wo], ld.at[5])
    load_wo.start()

    acc[...] = jnp.zeros_like(acc)
    sq[...] = jnp.zeros_like(sq)
    for cp in small:
        cp.wait()
    lengths = len_v[...].astype(F32)
    eye = lax.broadcasted_iota(jnp.int32, (ROWS, ROWS), 0) == lax.broadcasted_iota(
        jnp.int32, (ROWS, ROWS), 1
    )
    position = jnp.sum(jnp.where(eye, lengths, 0.0), axis=1, keepdims=True)
    lane = lax.broadcasted_iota(jnp.int32, (1, HD), 1)
    sign = jnp.where(lane < HD // 2, -1.0, 1.0)
    inverse = jnp.exp((lane & (HD // 2 - 1)).astype(F32) * (-math.log(1000000.0) / (HD // 2)))
    for s in range(STEPS):
        angle = (position + float(s)) * inverse
        cs[s] = jnp.cos(angle)
        sn[s] = jnp.sin(angle) * sign

    def mask(b, carry):
        rows = pl.ds(mult(b * 128, 128), 128)
        i = lax.broadcasted_iota(jnp.int32, (128, 1), 0) + b * 128
        r = i >> 4
        step = (i & 7) >> 1
        row_lane = lax.broadcasted_iota(jnp.int32, (1, ROWS), 1)
        limit = jnp.sum(jnp.where(row_lane == r + c * HALF, lengths, 0.0), axis=1, keepdims=True)
        place = lax.broadcasted_iota(jnp.int32, (1, CTX), 1).astype(F32)
        bias[rows, :] = jnp.where(place < limit, 0.0, -jnp.inf)
        n = lax.broadcasted_iota(jnp.int32, (1, 64), 1)
        usable = ((n & 15) == (r & 15)) & ((n >> 4) <= step)
        bias_f[rows, :] = jnp.where(usable, 0.0, -jnp.inf)
        return carry

    lax.fori_loop(0, 4, mask, 0)

    def project(i, carry):
        ks = pl.ds(mult(i * CHUNK, CHUNK), CHUNK)
        wait_chunk(i)
        g = gain[:, ks]
        for s in range(STEPS):
            xs = xv[s, :, :, :, ks].reshape(ROWS, CHUNK).astype(F32)
            ybf[s] = (xs * g).astype(BF)
            xx = xs * xs
            total = xx[:, 0:128]
            for j in range(1, CHUNK // 128):
                total = total + xx[:, j * 128:(j + 1) * 128]
            sq[s] += total
        acc[...] += jnp.dot(
            ybf[...].reshape(STEPS * ROWS, CHUNK), w[ks, :], preferred_element_type=F32
        )
        return carry

    lax.fori_loop(0, 2, project, 0)

    best = dist[0] * 8
    for i in range(1, 8):
        best = jnp.minimum(best, dist[i] * 8 + i)
    chosen = lax.rem(best, 8)

    def order(t, carry):
        ordr[t] = hold[chosen, smap[t]]
        return carry

    pltpu.make_async_copy(hold, hold, ld.at[6]).wait()
    lax.fori_loop(0, 16, order, 0)

    pl.semaphore_wait(barrier, len(greet))

    def rows_of(xl_, xh_, y_, z_, c_):
        return pl.ds(mult(((xl_ * 4 + z_) * 16 + xh_ * 8 + y_ * 2 + c_) * 64, 64), 64)

    def to_ranks(source, rows, order_):
        groups = {}
        for k in order_:
            yk = ring(y, k)
            groups[k] = flag()
            for flip in (0, 1):
                if k or flip:
                    ck = (c, 1 - c)[flip]
                    send(source.at[yk * 2 + ck], nw.at[rows], dev(xl, xh, yk, z, ck), groups[k])
        return groups

    mine = rows_of(xl, xh, y, z, c)
    own_copies = to_ranks(ordr.at[pl.ds(mult(xh * 8, 8), 8)], mine, (0, 1, 3, 2))
    cross_copies = {}
    for k in (2, 1, 3, 0):
        cross_copies[k] = send(
            ordr.at[pl.ds((1 - xh) * 8 + ring(y, k) * 2, 2)],
            w1r.at[pl.ds(ring(y, k) * 2, 2)],
            cross,
        )
    nw[mine] = ordr[xh * 8 + y * 2 + c]
    wo_copy = send(wo_hbm.at[:, sib_cols], wo.at[my_wo], sibling)

    lax.fori_loop(2, 6, project, 0)

    def pair_of(xl_, xh_, k):
        return pl.ds(mult(((xl_ * 4 + z) * 16 + xh_ * 8 + ring(y, -k) * 2) * 64, 128), 128)

    slabs = {"0a": (xl, xh), "0b": (1 - xl, 1 - xh), "1a": (1 - xl, xh), "1b": (xl, 1 - xh)}
    z_groups = {name: (flag(), flag()) for name in slabs}
    last_z = flag()
    near_copies = {"a": {}, "b": {}}

    def around(name, k):
        ref = nw.at[pair_of(*slabs[name], k)]
        send(ref, ref, z_up, z_groups[name][0])
        send(ref, ref, z_down, z_groups[name][1])
        if name[0] == "0":
            near_copies[name[1]][k] = send(ref, ref, near)

    def onward(name):
        xl_, xh_ = slabs[name]
        arrived(z_groups[name][0])
        low = nw.at[pl.ds(mult(((xl_ * 4 + ring(z, -1)) * 16 + xh_ * 8) * 64, 256), 256)]
        send(low, low, z_up, last_z)
        arrived(z_groups[name][1])
        high = nw.at[pl.ds(mult(((xl_ * 4 + ring(z, 1)) * 16 + xh_ * 8) * 64 + 256, 256), 256)]
        send(high, high, z_down, last_z)

    theirs = rows_of(1 - xl, 1 - xh, y, z, c)
    theirs_copies = {}

    def serve_theirs(k):
        arrived(cross_copies[k])
        if k == 0:
            nw[theirs] = w1r[y * 2 + c]
        theirs_copies.update(to_ranks(w1r, theirs, (k,)))

    def first_around(k):
        arrived(own_copies[k])
        around("0a", k)

    def second_around(k):
        arrived(theirs_copies[k])
        around("0b", k)

    def near_around(part_, k):
        arrived(near_copies[part_][k])
        around("1" + part_, k)

    lax.fori_loop(6, NCHUNK, project, 0)
    first_around(0)

    def turn(v, s):
        return v * cs[s] + pltpu.roll(v, HD // 2, 1) * sn[s]

    for s in range(STEPS):
        scale = lax.rsqrt(jnp.sum(sq[s], axis=1, keepdims=True) * (1.0 / WIDTH) + 1e-06)
        block = pl.ds(s * ROWS, ROWS)
        for h in range(2):
            cols = slice(h * HD, (h + 1) * HD)
            qs[s, :, cols] = turn(acc[block, cols] * scale, s).astype(BF)
        kn[s] = turn(acc[block, 256:384] * scale, s).astype(BF)
        vn[s] = (acc[block, 384:512] * scale).astype(BF)

    sib_half = pl.ds(mult((1 - c) * HALF, HALF), HALF)
    q_copy = send(qs.at[:, sib_half, :], qr, sibling)
    for s in range(STEPS):
        for h in range(2):
            qf[pl.ds(s * 2 + h, HALF, stride=16), :] = qs[s, my_half, h * HD:(h + 1) * HD].astype(
                F32
            )

    for k in (1, 3, 2):
        first_around(k)
    arrived(q_copy)
    for s in range(STEPS):
        for h in range(2):
            qf[pl.ds(8 + s * 2 + h, HALF, stride=16), :] = qr[s, :, h * HD:(h + 1) * HD].astype(F32)
    load_kv.wait()

    factor = 1.0 / math.sqrt(HD)

    def attend(b):
        block = pl.ds(b * 256, 256)
        sub = pl.ds(mult(c * HALF + b * 16, 16), 16)

        def score(i, carry):
            rows = pl.ds(mult(b * 256 + i * 16, 16), 16)
            mine_ = pl.ds(mult(i * 16, 16), 16)
            bias_here = bias[rows, :]
            got = lax.dot_general(
                qf[rows, :].astype(BF), kv[b * 16 + i, :, 0:HD], (((1,), (1,)), ((), ())),
                preferred_element_type=F32,
            )
            bias[rows, :] = got * factor + bias_here
            return carry

        lax.fori_loop(0, 16, score, 0, unroll=8)
        keys = kn[:, sub, :].reshape(STEPS * 16, HD)
        for part_of in range(2):
            rows = pl.ds(b * 256 + part_of * 128, 128)
            fresh = lax.dot_general(
                qf[rows, :].astype(BF), keys, (((1,), (1,)), ((), ())), preferred_element_type=F32
            ) * factor + bias_f[rows, :]
            cached = bias[rows, :]
            top = jnp.maximum(
                jnp.max(cached, axis=1, keepdims=True), jnp.max(fresh, axis=1, keepdims=True)
            )
            ce = jnp.exp(cached - top)
            fe = jnp.exp(fresh - top)
            total = jnp.sum(ce, axis=1, keepdims=True) + jnp.sum(fe, axis=1, keepdims=True)
            share = 1.0 / total
            pw[rows, :] = (ce * share).astype(BF)
            pf[rows, :] = (fe * share).astype(BF)
        values = vn[:, sub, :].reshape(STEPS * 16, HD)
        mix[block, :] = jnp.dot(pf[block, :], values, preferred_element_type=F32)

        def weigh(i, carry):
            rows = pl.ds(mult(b * 256 + i * 16, 16), 16)
            mix[rows, :] += jnp.dot(
                pw[rows, :], kv[b * 16 + i, :, HD:2 * HD], preferred_element_type=F32
            )
            return carry

        lax.fori_loop(0, 16, weigh, 0, unroll=8)
        for source in range(2):
            for s in range(STEPS):
                for h in range(2):
                    base = (c if source == 0 else 1 - c) * 256 + h * HD
                    att[b, s, c, :, pl.ds(mult(base, HD), HD)] = mix[
                        pl.ds(b * 256 + source * 8 + s * 2 + h, 16, stride=16), :
                    ].astype(BF)
        return send(att.at[b, :, c], att.at[b, :, c], sibling)

    def block_cols(yk, side):
        return pl.ds(mult(yk * 1024 + side * 512, 512), 512)

    def term(b, yk, side):
        cols = block_cols(yk, side)
        part[b, :, cols] = jnp.dot(
            att[b].reshape(128, 512), wo[:, cols], preferred_element_type=F32
        ).astype(BF)

    def piece(u, yk, side):
        return part.at[u // 2, pl.ds(u % 2 * 64, 64), block_cols(yk, side)]

    up, down, far = ring(y, 1), ring(y, -1), ring(y, 2)
    to_up, to_down, to_far = same_core(1), same_core(-1), same_core(2)
    o, n = 1 - xh, xh

    att_0 = attend(0)

    serve_theirs(2)
    serve_theirs(1)

    load_wo.wait()
    arrived(wo_copy)
    arrived(att_0)
    relay_up, relay_dn, direct_o, direct_n, a_across = {}, {}, {}, {}, {}
    b_copies, b2 = {}, flag()

    def start_relays(u):
        relay_up[u] = send(piece(u, far, o), rel_up.at[u - 1], to_up, lane=3)
        relay_dn[u] = send(piece(u, far, n), rel_dn.at[u - 1], to_down, lane=3)

    def start_direct(u):
        direct_o[u], direct_n[u] = flag(), flag()
        send(piece(u, down, o), dir_o.at[u - 1], to_down, direct_o[u], 3)
        send(piece(u, up, n), dir_n.at[u - 1], to_up, direct_n[u], 3)

    def start_b(k):
        b_copies[k] = send(piece(0, ring(y, k), o), rbx.at[k], across, lane=3)

    term(0, far, o)
    term(0, far, n)
    start_relays(1)
    start_b(2)
    term(0, down, o)
    term(0, up, n)
    start_direct(1)
    start_b(3)
    term(0, up, o)
    start_b(1)
    term(0, y, o)
    start_b(0)
    term(0, down, n)
    term(0, y, n)

    att_1 = attend(1)

    serve_theirs(3)
    serve_theirs(0)
    near_around("a", 0)

    def relay_sums(u):
        arrived(relay_up[u])
        s_up[u - 1] = (
            piece(u, up, o)[...].astype(F32) + rel_up[u - 1].astype(F32)
        ).astype(BF)
        send(s_up.at[u - 1], sum_o.at[u - 1], to_up, direct_o[u], 3)
        arrived(relay_dn[u])
        s_dn[u - 1] = (
            piece(u, down, n)[...].astype(F32) + rel_dn[u - 1].astype(F32)
        ).astype(BF)
        send(s_dn.at[u - 1], sum_n.at[u - 1], to_down, direct_n[u], 3)

    relay_sums(1)
    arrived(att_1)
    term(1, far, o)
    term(1, far, n)
    start_relays(2)
    start_relays(3)
    term(1, down, o)
    term(1, up, n)
    start_direct(2)
    start_direct(3)
    term(1, up, o)
    term(1, down, n)
    term(1, y, o)
    term(1, y, n)

    def pass_on(k):
        arrived(b_copies[k])
        sb[k - 1] = (
            piece(0, ring(y, k), n)[...].astype(F32) + rbx[k].astype(F32)
        ).astype(BF)
        send(sb.at[k - 1], rb.at[k - 1], same_core(k), b2, 3)

    def own_sums(u):
        arrived(direct_o[u])
        sa[u - 1] = (
            piece(u, y, o)[...].astype(F32)
            + dir_o[u - 1].astype(F32)
            + sum_o[u - 1].astype(F32)
        ).astype(BF)
        a_across[u] = send(sa.at[u - 1], rax.at[u - 1], across, lane=3)
        arrived(direct_n[u])
        keep_a[u - 1] = (
            piece(u, y, n)[...].astype(F32)
            + dir_n[u - 1].astype(F32)
            + sum_n[u - 1].astype(F32)
        )

    pass_on(2)
    second_around(2)
    second_around(1)
    near_around("a", 1)
    near_around("a", 3)
    near_around("a", 2)
    pass_on(3)
    second_around(3)
    second_around(0)
    pass_on(1)
    own_sums(1)
    relay_sums(2)
    arrived(b_copies[0])
    keep_b[...] = piece(0, y, n)[...].astype(F32) + rbx[0].astype(F32)
    relay_sums(3)
    onward("0a")

    def chunk_at(c_, y_, xh_, off=0, size=512):
        return pl.ds(mult(c_ * COLS + y_ * 1024 + xh_ * 512 + off, 128), size)

    def give(u, cols, *wheres):
        ref = out.at[pl.ds(u % 2 * 2, 2), :, u // 2, :, cols]
        return [send(ref, ref, where, lane=1) for where in wheres]

    to_sibling = flag()

    def share(u, cols):
        ref = out.at[pl.ds(u % 2 * 2, 2), :, u // 2, :, cols]
        send(ref, ref, sibling, to_sibling, 2)

    def finish(u, total):
        cols = chunk_at(c, y, xh)
        steps = pl.ds(u % 2 * 2, 2)
        whole = xv[steps, :, u // 2, :, cols].astype(F32) + total.reshape(2, 2, 16, 512)
        out[steps, :, u // 2, :, cols] = whole.astype(BF)

    own = chunk_at(c, y, xh)
    other = chunk_at(c, y, 1 - xh)
    ga, oa, near_parts, far_parts = {}, {}, {}, {}

    def finish_a(u):
        arrived(a_across[u])
        finish(u, keep_a[u - 1] + rax[u - 1].astype(F32))
        ga[u] = give(u, own, across, to_up, to_down)
        share(u, own)

    def other_block(u):
        arrived(ga[u][0])
        oa[u] = give(u, other, to_up, to_down)
        share(u, other)

    def relay(u, i_up, i_dn, side):
        group = flag()
        arrived(i_up)
        ref = out.at[pl.ds(u % 2 * 2, 2), :, u // 2, :, chunk_at(c, down, side, 0, 256)]
        send(ref, ref, to_up, group, 1)
        arrived(i_dn)
        ref = out.at[pl.ds(u % 2 * 2, 2), :, u // 2, :, chunk_at(c, up, side, 256, 256)]
        send(ref, ref, to_down, group, 1)
        share(u, chunk_at(c, down, side))
        share(u, chunk_at(c, up, side))
        return group

    def last_of(u, group, side):
        arrived(group)
        share(u, chunk_at(c, far, side))

    own_sums(2)
    finish_a(1)
    own_sums(3)
    for k in (2, 1, 3, 0):
        near_around("b", k)
    arrived(b2)
    finish(0, keep_b[...] + rb[0].astype(F32) + rb[1].astype(F32) + rb[2].astype(F32))
    gb_far, gb_up, gb_dn, gb_x = give(0, own, to_far, to_up, to_down, across)
    share(0, own)
    finish_a(2)
    near_parts[1] = relay(1, ga[1][1], ga[1][2], xh)
    other_block(1)
    finish_a(3)
    onward("0b")
    onward("1a")

    last = []

    def to_across(i, yk):
        arrived(i)
        cols = chunk_at(c, yk, xh)
        (j,) = give(0, cols, across)
        last.append((j, chunk_at(c, yk, 1 - xh)))
        share(0, cols)

    to_across(gb_up, down)
    to_across(gb_dn, up)
    near_parts[2] = relay(2, ga[2][1], ga[2][2], xh)
    other_block(2)
    to_across(gb_far, far)
    near_parts[3] = relay(3, ga[3][1], ga[3][2], xh)
    other_block(3)
    far_parts[1] = relay(1, oa[1][0], oa[1][1], 1 - xh)
    onward("1b")
    arrived(gb_x)
    share(0, other)
    last_of(1, near_parts[1], xh)
    far_parts[2] = relay(2, oa[2][0], oa[2][1], 1 - xh)
    last_of(2, near_parts[2], xh)
    far_parts[3] = relay(3, oa[3][0], oa[3][1], 1 - xh)
    last_of(1, far_parts[1], 1 - xh)
    last_of(3, near_parts[3], xh)
    for i, cols in last:
        arrived(i)
        share(0, cols)
    last_of(2, far_parts[2], 1 - xh)
    last_of(3, far_parts[3], 1 - xh)

    assert len(used) <= NCOPY
    for i in list(pending):
        arrived(i)
    for lane_, amount in enumerate(sent):
        wait_kib(ssem.at[lane_], amount)


def store(out_ref, nw_ref, out_hbm, nw_hbm, sem):
    copies = [
        pltpu.make_async_copy(out_ref, out_hbm, sem.at[0]),
        pltpu.make_async_copy(nw_ref, nw_hbm, sem.at[1]),
    ]
    for cp in copies:
        cp.start()
    for cp in copies:
        cp.wait()


def on_device(
    inputs, norm_gain, w_query, w_kv, w_out, kv_cache, kv_lengths, reuse_dist, shard_map,
    holder_weights,
):
    hbm = pl.BlockSpec(memory_space=pltpu.HBM)
    vmem = pl.BlockSpec(memory_space=pltpu.VMEM)
    dma = pltpu.SemaphoreType.DMA
    block = (64, 512)
    outputs, next_weights = pl.pallas_call(
        kernel,
        out_shape=(
            pltpu.VMEM((STEPS, 2, 2, 16, WIDTH), BF),
            pltpu.VMEM((WIDTH, 256), BF),
        ),
        in_specs=[hbm] * 10,
        out_specs=(vmem, vmem),
        scratch_shapes=[
            pltpu.VMEM((1, WIDTH), F32),
            pltpu.VMEM((1, ROWS), jnp.int32),
            pltpu.SMEM((8,), jnp.int32),
            pltpu.SMEM((16,), jnp.int32),
            pltpu.VMEM((STEPS, 2, 2, 16, WIDTH), BF),
            pltpu.VMEM((WIDTH, 512), BF),
            pltpu.VMEM((512, COLS), BF),
            pltpu.VMEM((HALF, CTX, 2 * HD), BF),
            pltpu.VMEM((8, 16, 64, 256), BF),
            pltpu.VMEM((16, 64, 256), BF),
            pltpu.VMEM((8, 64, 256), BF),
            pltpu.VMEM((STEPS * ROWS, 512), F32),
            pltpu.VMEM((STEPS, ROWS, 128), F32),
            pltpu.VMEM((STEPS, ROWS, CHUNK), BF),
            pltpu.VMEM((STEPS, ROWS, HD), F32),
            pltpu.VMEM((STEPS, ROWS, HD), F32),
            pltpu.VMEM((STEPS, ROWS, 256), BF),
            pltpu.VMEM((STEPS, HALF, 256), BF),
            pltpu.VMEM((STEPS, ROWS, HD), BF),
            pltpu.VMEM((STEPS, ROWS, HD), BF),
            pltpu.VMEM((512, HD), F32),
            pltpu.VMEM((512, CTX), F32),
            pltpu.VMEM((512, 64), F32),
            pltpu.VMEM((512, CTX), BF),
            pltpu.VMEM((512, 64), BF),
            pltpu.VMEM((512, HD), F32),
            pltpu.VMEM((2, STEPS, 2, 16, 512), BF),
            pltpu.VMEM((2, 128, COLS), BF),
            pltpu.VMEM((4,) + block, BF),
            pltpu.VMEM((3,) + block, BF),
            pltpu.VMEM((3,) + block, BF),
            pltpu.VMEM(block, F32),
            pltpu.VMEM((3,) + block, BF),
            pltpu.VMEM((3,) + block, BF),
            pltpu.VMEM((3,) + block, BF),
            pltpu.VMEM((3,) + block, BF),
            pltpu.VMEM((3,) + block, BF),
            pltpu.VMEM((3,) + block, BF),
            pltpu.VMEM((3,) + block, BF),
            pltpu.VMEM((3,) + block, BF),
            pltpu.VMEM((3,) + block, BF),
            pltpu.VMEM((3,) + block, BF),
            pltpu.VMEM((3,) + block, F32),
            dma((7,)),
            dma((NCHUNK, 2)),
            dma((4,)),
            dma((NCOPY,)),
        ],
        compiler_params=pltpu.CompilerParams(
            collective_id=0, has_side_effects=True, vmem_limit_bytes=48 * 1024 * 1024
        ),
    )(
        inputs.reshape(STEPS, 2, 2, 16, WIDTH), norm_gain.reshape(1, WIDTH), w_query, w_kv, w_out,
        kv_cache, kv_lengths.reshape(1, ROWS), reuse_dist, shard_map, holder_weights,
    )
    outputs, next_weights = pl.pallas_call(
        store,
        out_shape=(
            pltpu.HBM((STEPS, 2, 2, 16, WIDTH), BF),
            pltpu.HBM((WIDTH, 256), BF),
        ),
        in_specs=[vmem, vmem],
        out_specs=(hbm, hbm),
        scratch_shapes=[dma((2,))],
        compiler_params=pltpu.CompilerParams(vmem_limit_bytes=4 * 1024 * 1024),
    )(
        pltpu.with_memory_space_constraint(outputs, pltpu.VMEM),
        pltpu.with_memory_space_constraint(next_weights, pltpu.VMEM),
    )
    return outputs.reshape(STEPS, ROWS, WIDTH), next_weights


def solution(mesh):
    in_specs = (
        P(None, "dp", None),
        P(),
        P(None, "tensor"),
        P(None, "tensor"),
        P("tensor", None),
        P("dp", "tensor", None, None),
        P("dp"),
        P(),
        P(),
        P(None, ("dp", "tensor"), None),
    )
    out_specs = (P(None, "dp", None), P(None, "tensor"))
    return jax.shard_map(
        on_device, mesh=mesh, in_specs=in_specs, out_specs=out_specs, check_vma=False
    )
```

```python
import functools
import math

import jax
import jax.numpy as jnp
from jax import lax
from jax.experimental import pallas as pl
from jax.experimental.pallas import tpu as pltpu
from jax.sharding import PartitionSpec as P

MESH = pl.DeviceIdType.MESH
HD = 128
STEPS = 4
ROWS = 64
HALF = 32
WIDTH = 8192
CHUNK = 1024
NCHUNK = WIDTH // CHUNK
COLS = 4096
CTX = 256
NCOPY = 96
GROUPS = (
    (0, 0, 2, "A"),
    (0, 2, 2, "Br"),
    (1, 0, 2, "A"),
    (1, 2, 1, "A"),
    (1, 3, 1, "B"),
)
ORDER = (
    "W.f1", "W.f3", "attend0", "W.f2", "W.s2", "W.s1", "W.a0", "attend1", "g1.bf", "g1.bd",
    "g0.relay", "g0.direct", "g1.bo", "g2.relay", "g4.bf", "g4.bd", "g4.bo", "g4.bu", "g3.relay",
    "g1.bu", "g3.direct", "W.s0", "g2.direct", "W.a1", "W.s3", "W.q2", "W.a3", "W.q1", "W.q0",
    "g0.sumd", "g0.sumu", "g1.pf", "g2.sumu", "g1.po", "g2.sumd", "g3.sumd", "g4.pf", "g3.sumu",
    "g4.pd", "g4.po", "W.o0a", "g4.pu", "W.q3", "g0.o", "g1.pu", "W.b2", "g0.n", "g1.pd", "g2.o",
    "W.a2", "g2.n", "g3.o", "W.b1", "g3.n", "W.b0", "g4.fin", "W.b3", "W.o0b", "g1.fin",
    "g0.fino", "W.o1a", "g0.finn", "g4.af", "g4.ad", "g4.au", "g2.fino", "g1.ad", "g1.au",
    "g2.finn", "g3.fino", "W.o1b", "g0.rod", "g3.finn", "g0.rou", "g4.lx", "g0.rnu", "g0.rnd",
    "g1.lx", "g2.rod", "g2.rou", "g4.lf", "g1.af", "g4.ld", "g4.lu", "g2.rnu", "g2.rnd", "g3.rou",
    "g1.ld", "g3.rod", "g3.rnu", "g3.rnd", "g0.lo", "g1.lu", "g0.ln", "g2.lo", "g1.lf", "g2.ln",
    "g3.lo", "g3.ln",
)
BF = jnp.bfloat16
F32 = jnp.float32


def mult(value, by):
    return pl.multiple_of(value, by)


def kernel(
    x_hbm, gain_hbm, wq_hbm, wkv_hbm, wo_hbm, kv_hbm, len_hbm, dist_hbm, smap_hbm, hold_hbm,
    out, nw,
    gain, len_v, dist, smap,
    xv, w, wo, kv, hold, ordr, w1r, acc, sq, ybf, cs, sn, qs, qr, kn, vn, qf, bias, bias_f,
    pw, pf, mix, att, part, rbx, rb, sb, rel_up, rel_dn, dir_o, dir_n, sum_o, sum_n,
    s_up, s_dn, sa, rax, rbh, keep,
    ld, chunk_sem, ssem, rsem,
):
    dp = lax.axis_index("dp")
    tensor = lax.axis_index("tensor")
    xl, z = dp // 4, lax.rem(dp, 4)
    xh, y, c = tensor // 8, lax.rem(tensor // 2, 4), lax.rem(tensor, 2)

    def dev(xl_, xh_, y_, z_, c_):
        return (xl_ * 4 + z_, xh_ * 8 + y_ * 2 + c_)

    def ring(value, by):
        return lax.rem(value + by + 4, 4)

    used, sent, pending = [], [0, 0, 0, 0], {}

    def flag():
        used.append(0)
        return len(used) - 1

    def kib(ref):
        return math.prod(ref.shape) * 2 // 1024

    def send(src, dst, where, group=None, lane=0):
        i = flag() if group is None else group
        pltpu.make_async_remote_copy(
            src_ref=src, dst_ref=dst, send_sem=ssem.at[lane], recv_sem=rsem.at[i],
            device_id=where, device_id_type=MESH,
        ).start()
        sent[lane] += kib(src)
        pending[i] = pending.get(i, 0) + kib(dst)
        return i

    def wait_kib(sem, amount):
        ref = w.at[pl.ds(0, amount)]
        pltpu.make_async_copy(ref, ref, sem).wait()

    def arrived(i):
        wait_kib(rsem.at[i], pending.pop(i))

    sibling = dev(xl, xh, y, z, 1 - c)
    across = dev(xl, 1 - xh, y, z, c)
    cross = dev(1 - xl, 1 - xh, y, z, c)
    near = dev(1 - xl, xh, y, z, c)
    z_up = dev(xl, xh, y, ring(z, 1), c)
    z_down = dev(xl, xh, y, ring(z, -1), c)

    def same_core(k):
        return dev(xl, xh, ring(y, k), z, c)

    barrier = pltpu.get_barrier_semaphore()
    greet = [sibling, across, cross, near, z_up, z_down]
    for k in (1, 2, 3):
        for other in (c, 1 - c):
            greet.append(dev(xl, xh, ring(y, k), z, other))
    for where in greet:
        pl.semaphore_signal(barrier, inc=1, device_id=where, device_id_type=MESH)

    small = [
        pltpu.make_async_copy(a, b, ld.at[i])
        for i, (a, b) in enumerate(
            ((len_hbm, len_v), (gain_hbm, gain), (dist_hbm, dist), (smap_hbm, smap))
        )
    ]
    for cp in small:
        cp.start()

    def load_x(i):
        ks = pl.ds(mult(i * CHUNK, CHUNK), CHUNK)
        return pltpu.make_async_copy(
            x_hbm.at[:, :, :, :, ks], xv.at[:, :, :, :, ks], chunk_sem.at[i, 0]
        )

    def load_wq(i):
        ks = pl.ds(mult(i * CHUNK, CHUNK), CHUNK)
        return pltpu.make_async_copy(wq_hbm.at[ks], w.at[ks, pl.ds(0, 256)], chunk_sem.at[i, 1])

    def load_wkv(i):
        ks = pl.ds(mult(i * CHUNK, CHUNK), CHUNK)
        return pltpu.make_async_copy(wkv_hbm.at[ks], w.at[ks, pl.ds(256, 256)], chunk_sem.at[i, 2])

    def start_chunk(i, carry):
        load_x(i).start()
        load_wq(i).start()
        load_wkv(i).start()
        return carry

    def start_hold(t, carry):
        cols = pl.ds(mult(t * 256, 256), 256)
        pltpu.make_async_copy(hold_hbm.at[:, :, cols], hold.at[:, t], ld.at[6]).start()
        return carry

    lax.fori_loop(0, 2, start_chunk, 0)
    lax.fori_loop(0, 16, start_hold, 0)
    lax.fori_loop(2, NCHUNK, start_chunk, 0)
    my_half = pl.ds(mult(c * HALF, HALF), HALF)
    load_kv = pltpu.make_async_copy(kv_hbm.at[my_half, 0], kv, ld.at[4])
    load_kv.start()
    my_cols = pl.ds(mult(c * COLS, COLS), COLS)
    sib_cols = pl.ds(mult((1 - c) * COLS, COLS), COLS)
    my_wo = pl.ds(mult(c * 256, 256), 256)
    load_wo = pltpu.make_async_copy(wo_hbm.at[:, my_cols], wo.at[my_wo], ld.at[5])
    load_wo.start()

    acc[...] = jnp.zeros_like(acc)
    sq[...] = jnp.zeros_like(sq)
    for cp in small:
        cp.wait()
    lengths = len_v[...].astype(F32)
    eye = lax.broadcasted_iota(jnp.int32, (ROWS, ROWS), 0) == lax.broadcasted_iota(
        jnp.int32, (ROWS, ROWS), 1
    )
    position = jnp.sum(jnp.where(eye, lengths, 0.0), axis=1, keepdims=True)
    lane = lax.broadcasted_iota(jnp.int32, (1, HD), 1)
    sign = jnp.where(lane < HD // 2, -1.0, 1.0)
    inverse = jnp.exp((lane & (HD // 2 - 1)).astype(F32) * (-math.log(1000000.0) / (HD // 2)))
    for s in range(STEPS):
        angle = (position + float(s)) * inverse
        cs[s] = jnp.cos(angle)
        sn[s] = jnp.sin(angle) * sign

    def mask(b, carry):
        rows = pl.ds(mult(b * 128, 128), 128)
        i = lax.broadcasted_iota(jnp.int32, (128, 1), 0) + b * 128
        r = i >> 4
        step = (i & 7) >> 1
        row_lane = lax.broadcasted_iota(jnp.int32, (1, ROWS), 1)
        limit = jnp.sum(jnp.where(row_lane == r + c * HALF, lengths, 0.0), axis=1, keepdims=True)
        place = lax.broadcasted_iota(jnp.int32, (1, CTX), 1).astype(F32)
        bias[rows, :] = jnp.where(place < limit, 0.0, -jnp.inf)
        n = lax.broadcasted_iota(jnp.int32, (1, 64), 1)
        usable = ((n & 15) == (r & 15)) & ((n >> 4) <= step)
        bias_f[rows, :] = jnp.where(usable, 0.0, -jnp.inf)
        return carry

    lax.fori_loop(0, 4, mask, 0)

    def project(i, carry):
        ks = pl.ds(mult(i * CHUNK, CHUNK), CHUNK)
        load_x(i).wait()
        load_wq(i).wait()
        load_wkv(i).wait()
        g = gain[:, ks]
        for s in range(STEPS):
            xs = xv[s, :, :, :, ks].reshape(ROWS, CHUNK).astype(F32)
            ybf[s] = (xs * g).astype(BF)
            xx = xs * xs
            total = xx[:, 0:128]
            for j in range(1, CHUNK // 128):
                total = total + xx[:, j * 128:(j + 1) * 128]
            sq[s] += total
        acc[...] += jnp.dot(
            ybf[...].reshape(STEPS * ROWS, CHUNK), w[ks, :], preferred_element_type=F32
        )
        return carry

    lax.fori_loop(0, 2, project, 0)

    best = dist[0] * 8
    for i in range(1, 8):
        best = jnp.minimum(best, dist[i] * 8 + i)
    chosen = lax.rem(best, 8)

    def order(t, carry):
        ordr[t] = hold[chosen, smap[t]]
        return carry

    pltpu.make_async_copy(hold, hold, ld.at[6]).wait()
    lax.fori_loop(0, 16, order, 0)

    pl.semaphore_wait(barrier, len(greet))

    def rows_of(xl_, xh_, y_, z_, c_):
        return pl.ds(mult(((xl_ * 4 + z_) * 16 + xh_ * 8 + y_ * 2 + c_) * 64, 64), 64)

    def to_ranks(source, rows, order_):
        groups = {}
        for k in order_:
            yk = ring(y, k)
            groups[k] = flag()
            for flip in (0, 1):
                if k or flip:
                    ck = (c, 1 - c)[flip]
                    send(source.at[yk * 2 + ck], nw.at[rows], dev(xl, xh, yk, z, ck), groups[k])
        return groups

    mine = rows_of(xl, xh, y, z, c)
    own_copies = to_ranks(ordr.at[pl.ds(mult(xh * 8, 8), 8)], mine, (0, 1, 3, 2))
    cross_copies = {}
    for k in (2, 1, 3, 0):
        cross_copies[k] = send(
            ordr.at[pl.ds((1 - xh) * 8 + ring(y, k) * 2, 2)],
            w1r.at[pl.ds(ring(y, k) * 2, 2)],
            cross,
        )
    nw[mine] = ordr[xh * 8 + y * 2 + c]
    wo_copy = send(wo_hbm.at[:, sib_cols], wo.at[my_wo], sibling)

    lax.fori_loop(2, 6, project, 0)

    def pair_of(xl_, xh_, k):
        return pl.ds(mult(((xl_ * 4 + z) * 16 + xh_ * 8 + ring(y, -k) * 2) * 64, 128), 128)

    slabs = {"0a": (xl, xh), "0b": (1 - xl, 1 - xh), "1a": (1 - xl, xh), "1b": (xl, 1 - xh)}
    z_groups = {name: (flag(), flag()) for name in slabs}
    last_z = flag()
    near_copies = {"a": {}, "b": {}}

    def around(name, k):
        ref = nw.at[pair_of(*slabs[name], k)]
        send(ref, ref, z_up, z_groups[name][0])
        send(ref, ref, z_down, z_groups[name][1])
        if name[0] == "0":
            near_copies[name[1]][k] = send(ref, ref, near)

    def onward(name):
        xl_, xh_ = slabs[name]
        arrived(z_groups[name][0])
        low = nw.at[pl.ds(mult(((xl_ * 4 + ring(z, -1)) * 16 + xh_ * 8) * 64, 256), 256)]
        send(low, low, z_up, last_z)
        arrived(z_groups[name][1])
        high = nw.at[pl.ds(mult(((xl_ * 4 + ring(z, 1)) * 16 + xh_ * 8) * 64 + 256, 256), 256)]
        send(high, high, z_down, last_z)

    theirs = rows_of(1 - xl, 1 - xh, y, z, c)
    theirs_copies = {}

    def serve_theirs(k):
        arrived(cross_copies[k])
        if k == 0:
            nw[theirs] = w1r[y * 2 + c]
        theirs_copies.update(to_ranks(w1r, theirs, (k,)))

    def first_around(k):
        arrived(own_copies[k])
        around("0a", k)

    def second_around(k):
        arrived(theirs_copies[k])
        around("0b", k)

    def near_around(part_, k):
        arrived(near_copies[part_][k])
        around("1" + part_, k)

    first_around(0)
    lax.fori_loop(6, NCHUNK, project, 0)

    def turn(v, s):
        return v * cs[s] + pltpu.roll(v, HD // 2, 1) * sn[s]

    for s in range(STEPS):
        scale = lax.rsqrt(jnp.sum(sq[s], axis=1, keepdims=True) * (1.0 / WIDTH) + 1e-06)
        block = pl.ds(s * ROWS, ROWS)
        for h in range(2):
            cols = slice(h * HD, (h + 1) * HD)
            qs[s, :, cols] = turn(acc[block, cols] * scale, s).astype(BF)
        if s == STEPS - 1:
            sib_half = pl.ds(mult((1 - c) * HALF, HALF), HALF)
            q_copy = send(qs.at[:, sib_half, :], qr, sibling)
    for s in range(STEPS):
        scale = lax.rsqrt(jnp.sum(sq[s], axis=1, keepdims=True) * (1.0 / WIDTH) + 1e-06)
        block = pl.ds(s * ROWS, ROWS)
        kn[s] = turn(acc[block, 256:384] * scale, s).astype(BF)
        vn[s] = (acc[block, 384:512] * scale).astype(BF)

    for s in range(STEPS):
        for h in range(2):
            qf[pl.ds(s * 2 + h, HALF, stride=16), :] = qs[s, my_half, h * HD:(h + 1) * HD].astype(
                F32
            )

    factor = 1.0 / math.sqrt(HD)

    def attend(b):
        block = pl.ds(b * 256, 256)
        sub = pl.ds(mult(c * HALF + b * 16, 16), 16)

        def score(i, carry):
            rows = pl.ds(mult(b * 256 + i * 16, 16), 16)
            mine_ = pl.ds(mult(i * 16, 16), 16)
            bias_here = bias[rows, :]
            got = lax.dot_general(
                qf[rows, :].astype(BF), kv[b * 16 + i, :, 0:HD], (((1,), (1,)), ((), ())),
                preferred_element_type=F32,
            )
            bias[rows, :] = got * factor + bias_here
            return carry

        lax.fori_loop(0, 16, score, 0, unroll=8)
        keys = kn[:, sub, :].reshape(STEPS * 16, HD)
        for part_of in range(2):
            rows = pl.ds(b * 256 + part_of * 128, 128)
            fresh = lax.dot_general(
                qf[rows, :].astype(BF), keys, (((1,), (1,)), ((), ())), preferred_element_type=F32
            ) * factor + bias_f[rows, :]
            cached = bias[rows, :]
            top = jnp.maximum(
                jnp.max(cached, axis=1, keepdims=True), jnp.max(fresh, axis=1, keepdims=True)
            )
            ce = jnp.exp(cached - top)
            fe = jnp.exp(fresh - top)
            total = jnp.sum(ce, axis=1, keepdims=True) + jnp.sum(fe, axis=1, keepdims=True)
            share = 1.0 / total
            pw[rows, :] = (ce * share).astype(BF)
            pf[rows, :] = (fe * share).astype(BF)
        values = vn[:, sub, :].reshape(STEPS * 16, HD)
        mix[block, :] = jnp.dot(pf[block, :], values, preferred_element_type=F32)

        def weigh(i, carry):
            rows = pl.ds(mult(b * 256 + i * 16, 16), 16)
            mix[rows, :] += jnp.dot(
                pw[rows, :], kv[b * 16 + i, :, HD:2 * HD], preferred_element_type=F32
            )
            return carry

        lax.fori_loop(0, 16, weigh, 0, unroll=8)
        for source in range(2):
            for s in range(STEPS):
                for h in range(2):
                    base = (c if source == 0 else 1 - c) * 256 + h * HD
                    att[b, s, c, :, pl.ds(mult(base, HD), HD)] = mix[
                        pl.ds(b * 256 + source * 8 + s * 2 + h, 16, stride=16), :
                    ].astype(BF)
        return send(att.at[b, :, c], att.at[b, :, c], sibling)

    def block_cols(yk, side):
        return pl.ds(mult(yk * 1024 + side * 512, 512), 512)

    def term(b, yk, side):
        cols = block_cols(yk, side)
        part[b, :, cols] = jnp.dot(
            att[b].reshape(128, 512), wo[:, cols], preferred_element_type=F32
        ).astype(BF)

    up, down, far = ring(y, 1), ring(y, -1), ring(y, 2)
    to_up, to_down, to_far = same_core(1), same_core(-1), same_core(2)
    o, n = 1 - xh, xh


    tasks = {}
    for k in range(4):
        tasks[f"W.s{k}"] = functools.partial(serve_theirs, k)
        tasks[f"W.q{k}"] = functools.partial(second_around, k)
        tasks[f"W.a{k}"] = functools.partial(near_around, "a", k)
        tasks[f"W.b{k}"] = functools.partial(near_around, "b", k)
    for name in slabs:
        tasks["W.o" + name] = functools.partial(onward, name)

    att_copies = {}

    def attend_to(b):
        if b == 0:
            arrived(q_copy)
            for s in range(STEPS):
                for h in range(2):
                    qf[pl.ds(8 + s * 2 + h, HALF, stride=16), :] = qr[
                        s, :, h * HD:(h + 1) * HD
                    ].astype(F32)
            load_kv.wait()
        att_copies[b] = attend(b)

    for b in range(2):
        tasks[f"attend{b}"] = functools.partial(attend_to, b)
    for k in (1, 2, 3):
        tasks[f"W.f{k}"] = functools.partial(first_around, k)
    made, ready = set(), set()

    def need(b, *blocks):
        if not ready:
            load_wo.wait()
            arrived(wo_copy)
        if b not in ready:
            ready.add(b)
            arrived(att_copies[b])
        for name, yk, side in blocks:
            if (b, name) not in made:
                made.add((b, name))
                term(b, yk, side)

    block_of = {
        "fo": (far, o), "fn": (far, n), "uo": (up, o), "un": (up, n),
        "do": (down, o), "dn": (down, n), "o": (y, o), "n": (y, n),
    }
    to_sibling = flag()

    def chunk_at(c_, y_, xh_, off=0, size=512):
        return pl.ds(mult(c_ * COLS + y_ * 1024 + xh_ * 512 + off, 128), size)

    own = chunk_at(c, y, xh)
    other = chunk_at(c, y, 1 - xh)

    def add_group(g, b, step, steps, kind):
        rows = steps * 32
        span = pl.ds(step * 32, rows)
        f = {}

        def slot(ref, *index):
            return ref.at[(g,) + index + (pl.ds(0, rows),)]

        def mine_of(name):
            need(b, (name,) + block_of[name])
            return part.at[b, span, block_cols(*block_of[name])]

        def wide(ref):
            return ref[...].astype(F32)

        def out_at(cols):
            return out.at[pl.ds(step, steps), :, b, :, cols]

        def give(cols, where, group=None):
            return send(out_at(cols), out_at(cols), where, group, 1)

        def share(cols):
            send(out_at(cols), out_at(cols), sibling, to_sibling, 2)

        def finish(total, cols):
            ref = xv.at[pl.ds(step, steps), :, b, :, cols]
            out_at(cols)[...] = (wide(ref) + total.reshape(steps, 2, 16, 512)).astype(BF)

        def add(name, run):
            tasks[f"g{g}.{name}"] = run

        def relay():
            f["ru"] = send(mine_of("fo"), slot(rel_up), to_up, lane=3)
            f["rd"] = send(mine_of("fn"), slot(rel_dn), to_down, lane=3)

        def direct():
            f["o"], f["n"] = flag(), flag()
            send(mine_of("do"), slot(dir_o), to_down, f["o"], 3)
            send(mine_of("un"), slot(dir_n), to_up, f["n"], 3)

        def sum_up():
            first = wide(mine_of("uo"))
            arrived(f["ru"])
            slot(s_up)[...] = (first + wide(slot(rel_up))).astype(BF)
            send(slot(s_up), slot(sum_o), to_up, f["o"], 3)

        def sum_down():
            first = wide(mine_of("dn"))
            arrived(f["rd"])
            slot(s_dn)[...] = (first + wide(slot(rel_dn))).astype(BF)
            send(slot(s_dn), slot(sum_n), to_down, f["n"], 3)

        def own_sum(q, more, added):
            first = wide(mine_of(q))
            arrived(f[q])
            slot(sa, "no".index(q))[...] = (first + wide(more) + wide(added)).astype(BF)
            ref = slot(sa, "no".index(q))
            f["x" + q] = send(ref, slot(rax, "on".index(q)), across, lane=3)

        def finish_a(q, cols):
            arrived(f["x" + ("o" if q == "n" else "n")])
            i = "no".index(q)
            finish(wide(slot(sa, i)) + wide(slot(rax, i)), cols)
            f["gu" + q] = give(cols, to_up)
            f["gd" + q] = give(cols, to_down)
            share(cols)

        def half_up(q, side):
            arrived(f["gu" + q])
            if "h" + q not in f:
                f["h" + q] = flag()
            give(chunk_at(c, down, side, 0, 256), to_up, f["h" + q])
            share(chunk_at(c, down, side))

        def half_down(q, side):
            arrived(f["gd" + q])
            if "h" + q not in f:
                f["h" + q] = flag()
            give(chunk_at(c, up, side, 256, 256), to_down, f["h" + q])
            share(chunk_at(c, up, side))

        def last_far(q, side):
            arrived(f["h" + q])
            share(chunk_at(c, far, side))

        to = {"f": (far, to_far), "u": (up, to_up), "d": (down, to_down)}

        def start(k):
            cols = k + "o" if k in to else "o"
            f["x" + k] = send(mine_of(cols), slot(rbx, "fudo".index(k)), across, lane=3)

        def pass_on(k):
            first = wide(mine_of(k + "n"))
            arrived(f["x" + k])
            i = "fud".index(k)
            if "y" not in f:
                f["y"] = flag()
            if kind == "Br" and k == "f":
                slot(sb, i)[...] = (first + wide(slot(rbx, i))).astype(BF)
                f["hu"] = send(
                    slot(sb, i).at[:, pl.ds(0, 256)], slot(rbh, 0), to_up, lane=3
                )
                f["hd"] = send(
                    slot(sb, i).at[:, pl.ds(256, 256)], slot(rbh, 1), to_down, lane=3
                )
                return
            total = first + wide(slot(rbx, i))
            if kind == "Br":
                arrived(f["h" + k])
                if k == "u":
                    more = jnp.concatenate(
                        [total[:, :256] + wide(slot(rbh, 0)), total[:, 256:]], axis=1
                    )
                else:
                    more = jnp.concatenate(
                        [total[:, :256], total[:, 256:] + wide(slot(rbh, 1))], axis=1
                    )
                total = more
            slot(sb, i)[...] = total.astype(BF)
            send(slot(sb, i), slot(rb, i), to[k][1], f["y"], 3)

        def pass_own():
            first = wide(mine_of("n"))
            arrived(f["xo"])
            slot(keep)[...] = first + wide(slot(rbx, 3))

        def finish_b():
            arrived(f["y"])
            total = slot(keep)[...] + wide(slot(rb, 1)) + wide(slot(rb, 2))
            if kind == "B":
                total = total + wide(slot(rb, 0))
            finish(total, own)
            if kind == "B":
                f["gf"] = give(own, to_far)
            f["gu"] = give(own, to_up)
            f["gd"] = give(own, to_down)
            f["gx"] = give(own, across)
            share(own)

        source = {"f": far, "u": down, "d": up}

        def to_across(k):
            arrived(f["g" + k])
            if kind == "Br" and k != "f":
                if "gf" not in f:
                    f["gf"] = flag()
                if k == "u":
                    give(chunk_at(c, down, xh, 0, 256), to_up, f["gf"])
                else:
                    give(chunk_at(c, up, xh, 256, 256), to_down, f["gf"])
            f["z" + k] = give(chunk_at(c, source[k], xh), across)
            share(chunk_at(c, source[k], xh))

        def last_across(k):
            arrived(f["z" + k])
            share(chunk_at(c, source[k], 1 - xh))

        def last_own():
            arrived(f["gx"])
            share(other)

        if kind == "A":
            add("relay", relay)
            add("direct", direct)
            add("sumu", sum_up)
            add("sumd", sum_down)
            add("o", functools.partial(own_sum, "o", slot(dir_o), slot(sum_o)))
            add("n", functools.partial(own_sum, "n", slot(dir_n), slot(sum_n)))
            for q, side, cols in (("n", xh, own), ("o", 1 - xh, other)):
                add("fin" + q, functools.partial(finish_a, q, cols))
                add(f"r{q}u", functools.partial(half_up, q, side))
                add(f"r{q}d", functools.partial(half_down, q, side))
                add("l" + q, functools.partial(last_far, q, side))
        else:
            for k in "fudo":
                add("b" + k, functools.partial(start, k))
            for k in "fud":
                add("p" + k, functools.partial(pass_on, k))
                add("a" + k, functools.partial(to_across, k))
                add("l" + k, functools.partial(last_across, k))
            add("po", pass_own)
            add("fin", finish_b)
            add("lx", last_own)

    for g, spec in enumerate(GROUPS):
        add_group(g, *spec)
    assert sorted(ORDER) == sorted(tasks)
    for name in ORDER:
        tasks[name]()

    assert len(used) <= NCOPY
    for i in list(pending):
        arrived(i)
    for lane_, amount in enumerate(sent):
        wait_kib(ssem.at[lane_], amount)


def store(out_ref, nw_ref, out_hbm, nw_hbm, sem):
    copies = [
        pltpu.make_async_copy(out_ref, out_hbm, sem.at[0]),
        pltpu.make_async_copy(nw_ref, nw_hbm, sem.at[1]),
    ]
    for cp in copies:
        cp.start()
    for cp in copies:
        cp.wait()


def on_device(
    inputs, norm_gain, w_query, w_kv, w_out, kv_cache, kv_lengths, reuse_dist, shard_map,
    holder_weights,
):
    hbm = pl.BlockSpec(memory_space=pltpu.HBM)
    vmem = pl.BlockSpec(memory_space=pltpu.VMEM)
    dma = pltpu.SemaphoreType.DMA
    block = (len(GROUPS), 64, 512)
    outputs, next_weights = pl.pallas_call(
        kernel,
        out_shape=(
            pltpu.VMEM((STEPS, 2, 2, 16, WIDTH), BF),
            pltpu.VMEM((WIDTH, 256), BF),
        ),
        in_specs=[hbm] * 10,
        out_specs=(vmem, vmem),
        scratch_shapes=[
            pltpu.VMEM((1, WIDTH), F32),
            pltpu.VMEM((1, ROWS), jnp.int32),
            pltpu.SMEM((8,), jnp.int32),
            pltpu.SMEM((16,), jnp.int32),
            pltpu.VMEM((STEPS, 2, 2, 16, WIDTH), BF),
            pltpu.VMEM((WIDTH, 512), BF),
            pltpu.VMEM((512, COLS), BF),
            pltpu.VMEM((HALF, CTX, 2 * HD), BF),
            pltpu.VMEM((8, 16, 64, 256), BF),
            pltpu.VMEM((16, 64, 256), BF),
            pltpu.VMEM((8, 64, 256), BF),
            pltpu.VMEM((STEPS * ROWS, 512), F32),
            pltpu.VMEM((STEPS, ROWS, 128), F32),
            pltpu.VMEM((STEPS, ROWS, CHUNK), BF),
            pltpu.VMEM((STEPS, ROWS, HD), F32),
            pltpu.VMEM((STEPS, ROWS, HD), F32),
            pltpu.VMEM((STEPS, ROWS, 256), BF),
            pltpu.VMEM((STEPS, HALF, 256), BF),
            pltpu.VMEM((STEPS, ROWS, HD), BF),
            pltpu.VMEM((STEPS, ROWS, HD), BF),
            pltpu.VMEM((512, HD), F32),
            pltpu.VMEM((512, CTX), F32),
            pltpu.VMEM((512, 64), F32),
            pltpu.VMEM((512, CTX), BF),
            pltpu.VMEM((512, 64), BF),
            pltpu.VMEM((512, HD), F32),
            pltpu.VMEM((2, STEPS, 2, 16, 512), BF),
            pltpu.VMEM((2, 128, COLS), BF),
            pltpu.VMEM((len(GROUPS), 4, 64, 512), BF),
            pltpu.VMEM((len(GROUPS), 3, 64, 512), BF),
            pltpu.VMEM((len(GROUPS), 3, 64, 512), BF),
            pltpu.VMEM(block, BF),
            pltpu.VMEM(block, BF),
            pltpu.VMEM(block, BF),
            pltpu.VMEM(block, BF),
            pltpu.VMEM(block, BF),
            pltpu.VMEM(block, BF),
            pltpu.VMEM(block, BF),
            pltpu.VMEM(block, BF),
            pltpu.VMEM((len(GROUPS), 2, 64, 512), BF),
            pltpu.VMEM((len(GROUPS), 2, 64, 512), BF),
            pltpu.VMEM((len(GROUPS), 2, 64, 256), BF),
            pltpu.VMEM(block, F32),
            dma((7,)),
            dma((NCHUNK, 3)),
            dma((4,)),
            dma((NCOPY,)),
        ],
        compiler_params=pltpu.CompilerParams(
            collective_id=0, has_side_effects=True, vmem_limit_bytes=48 * 1024 * 1024
        ),
    )(
        inputs.reshape(STEPS, 2, 2, 16, WIDTH), norm_gain.reshape(1, WIDTH), w_query, w_kv, w_out,
        kv_cache, kv_lengths.reshape(1, ROWS), reuse_dist, shard_map, holder_weights,
    )
    outputs, next_weights = pl.pallas_call(
        store,
        out_shape=(
            pltpu.HBM((STEPS, 2, 2, 16, WIDTH), BF),
            pltpu.HBM((WIDTH, 256), BF),
        ),
        in_specs=[vmem, vmem],
        out_specs=(hbm, hbm),
        scratch_shapes=[dma((2,))],
        compiler_params=pltpu.CompilerParams(vmem_limit_bytes=4 * 1024 * 1024),
    )(
        pltpu.with_memory_space_constraint(outputs, pltpu.VMEM),
        pltpu.with_memory_space_constraint(next_weights, pltpu.VMEM),
    )
    return outputs.reshape(STEPS, ROWS, WIDTH), next_weights


def solution(mesh):
    in_specs = (
        P(None, "dp", None),
        P(),
        P(None, "tensor"),
        P(None, "tensor"),
        P("tensor", None),
        P("dp", "tensor", None, None),
        P("dp"),
        P(),
        P(),
        P(None, ("dp", "tensor"), None),
    )
    out_specs = (P(None, "dp", None), P(None, "tensor"))
    return jax.shard_map(
        on_device, mesh=mesh, in_specs=in_specs, out_specs=out_specs, check_vma=False
    )
```

```python
import functools
import math

import jax
import jax.numpy as jnp
from jax import lax
from jax.experimental import pallas as pl
from jax.experimental.pallas import tpu as pltpu
from jax.sharding import PartitionSpec as P

MESH = pl.DeviceIdType.MESH
HD = 128
STEPS = 4
ROWS = 64
HALF = 32
WIDTH = 8192
CHUNK = 1024
NCHUNK = WIDTH // CHUNK
COLS = 4096
CTX = 256
NCOPY = 96
GROUPS = (
    (0, 0, 2, "A"),
    (0, 2, 2, "Br"),
    (1, 0, 2, "A"),
    (1, 2, 1, "A"),
    (1, 3, 1, "B"),
)
ORDER = (
    "W.f1", "W.f3", "attend0", "W.f2", "W.s2", "W.s1", "W.a0", "attend1", "g1.bf", "g1.bd",
    "g0.relay", "g0.direct", "g1.bo", "g2.relay", "g4.bf", "g4.bd", "g4.bo", "g4.bu", "g3.relay",
    "g1.bu", "g3.direct", "W.s0", "g2.direct", "W.a1", "W.s3", "W.q2", "W.a3", "W.q1", "W.q0",
    "g0.sumd", "g0.sumu", "g1.pf", "g2.sumu", "g1.po", "g2.sumd", "g3.sumd", "g4.pf", "g3.sumu",
    "g4.pd", "g4.po", "W.o0a", "g4.pu", "W.q3", "g0.o", "g1.pu", "W.b2", "g0.n", "g1.pd", "g2.o",
    "W.a2", "g2.n", "g3.o", "W.b1", "g3.n", "W.b0", "g4.fin", "W.b3", "W.o0b", "g1.fin",
    "g0.fino", "W.o1a", "g0.finn", "g4.af", "g4.ad", "g4.au", "g2.fino", "g1.ad", "g1.au",
    "g2.finn", "g3.fino", "W.o1b", "g0.rod", "g3.finn", "g0.rou", "g4.lx", "g0.rnu", "g0.rnd",
    "g1.lx", "g2.rod", "g2.rou", "g4.lf", "g1.af", "g4.ld", "g4.lu", "g2.rnu", "g2.rnd", "g3.rou",
    "g1.ld", "g3.rod", "g3.rnu", "g3.rnd", "g0.lo", "g1.lu", "g0.ln", "g2.lo", "g1.lf", "g2.ln",
    "g3.lo", "g3.ln",
)
BF = jnp.bfloat16
F32 = jnp.float32


def mult(value, by):
    return pl.multiple_of(value, by)


def kernel(
    x_hbm, gain_hbm, wq_hbm, wkv_hbm, wo_hbm, kv_hbm, len_hbm, dist_hbm, smap_hbm, hold_hbm,
    out, nw,
    gain, len_v, dist, smap,
    xv, w, wo, kv, hold, ordr, w1r, acc, sq, ybf, cs, sn, qs, qr, kn, vn, qf, bias, bias_f,
    pw, pf, mix, att, part, rbx, rb, sb, rel_up, rel_dn, dir_o, dir_n, sum_o, sum_n,
    s_up, s_dn, sa, rax, rbh, keep,
    ld, chunk_sem, ssem, rsem,
):
    dp = lax.axis_index("dp")
    tensor = lax.axis_index("tensor")
    xl, z = dp // 4, lax.rem(dp, 4)
    xh, y, c = tensor // 8, lax.rem(tensor // 2, 4), lax.rem(tensor, 2)

    def dev(xl_, xh_, y_, z_, c_):
        return (xl_ * 4 + z_, xh_ * 8 + y_ * 2 + c_)

    def ring(value, by):
        return lax.rem(value + by + 4, 4)

    used, sent, pending = [], [0, 0, 0, 0], {}

    def flag():
        used.append(0)
        return len(used) - 1

    def kib(ref):
        return math.prod(ref.shape) * 2 // 1024

    def send(src, dst, where, group=None, lane=0):
        i = flag() if group is None else group
        pltpu.make_async_remote_copy(
            src_ref=src, dst_ref=dst, send_sem=ssem.at[lane], recv_sem=rsem.at[i],
            device_id=where, device_id_type=MESH,
        ).start()
        sent[lane] += kib(src)
        pending[i] = pending.get(i, 0) + kib(dst)
        return i

    def wait_kib(sem, amount):
        ref = w.at[pl.ds(0, amount)]
        pltpu.make_async_copy(ref, ref, sem).wait()

    def arrived(i):
        wait_kib(rsem.at[i], pending.pop(i))

    sibling = dev(xl, xh, y, z, 1 - c)
    across = dev(xl, 1 - xh, y, z, c)
    cross = dev(1 - xl, 1 - xh, y, z, c)
    near = dev(1 - xl, xh, y, z, c)
    z_up = dev(xl, xh, y, ring(z, 1), c)
    z_down = dev(xl, xh, y, ring(z, -1), c)

    def same_core(k):
        return dev(xl, xh, ring(y, k), z, c)

    barrier = pltpu.get_barrier_semaphore()
    greet = [across]
    for k in (2, 1, 3):
        for other in (1 - c, c):
            greet.append(dev(xl, xh, ring(y, k), z, other))
    greet += [z_up, z_down, cross, near, sibling]
    for where in greet:
        pl.semaphore_signal(barrier, inc=1, device_id=where, device_id_type=MESH)

    small = [
        pltpu.make_async_copy(a, b, ld.at[i])
        for i, (a, b) in enumerate(
            ((len_hbm, len_v), (gain_hbm, gain), (dist_hbm, dist), (smap_hbm, smap))
        )
    ]
    for cp in small:
        cp.start()

    def load_x(i):
        ks = pl.ds(mult(i * CHUNK, CHUNK), CHUNK)
        return pltpu.make_async_copy(
            x_hbm.at[:, :, :, :, ks], xv.at[:, :, :, :, ks], chunk_sem.at[i, 0]
        )

    def load_wq(i):
        ks = pl.ds(mult(i * CHUNK, CHUNK), CHUNK)
        return pltpu.make_async_copy(wq_hbm.at[ks], w.at[ks, pl.ds(0, 256)], chunk_sem.at[i, 1])

    def load_wkv(i):
        ks = pl.ds(mult(i * CHUNK, CHUNK), CHUNK)
        return pltpu.make_async_copy(wkv_hbm.at[ks], w.at[ks, pl.ds(256, 256)], chunk_sem.at[i, 2])

    def start_chunk(i, carry):
        load_x(i).start()
        load_wq(i).start()
        load_wkv(i).start()
        return carry

    def start_hold(t, carry):
        cols = pl.ds(mult(t * 256, 256), 256)
        pltpu.make_async_copy(hold_hbm.at[:, :, cols], hold.at[:, t], ld.at[6]).start()
        return carry

    lax.fori_loop(0, 2, start_chunk, 0)
    lax.fori_loop(0, 16, start_hold, 0)
    lax.fori_loop(2, NCHUNK, start_chunk, 0)
    my_half = pl.ds(mult(c * HALF, HALF), HALF)
    load_kv = pltpu.make_async_copy(kv_hbm.at[my_half, 0], kv, ld.at[4])
    load_kv.start()
    my_cols = pl.ds(mult(c * COLS, COLS), COLS)
    sib_cols = pl.ds(mult((1 - c) * COLS, COLS), COLS)
    my_wo = pl.ds(mult(c * 256, 256), 256)
    load_wo = pltpu.make_async_copy(wo_hbm.at[:, my_cols], wo.at[my_wo], ld.at[5])
    load_wo.start()

    acc[...] = jnp.zeros_like(acc)
    sq[...] = jnp.zeros_like(sq)
    for cp in small:
        cp.wait()
    lengths = len_v[...].astype(F32)
    eye = lax.broadcasted_iota(jnp.int32, (ROWS, ROWS), 0) == lax.broadcasted_iota(
        jnp.int32, (ROWS, ROWS), 1
    )
    position = jnp.sum(jnp.where(eye, lengths, 0.0), axis=1, keepdims=True)
    lane = lax.broadcasted_iota(jnp.int32, (1, HD), 1)
    sign = jnp.where(lane < HD // 2, -1.0, 1.0)
    inverse = jnp.exp((lane & (HD // 2 - 1)).astype(F32) * (-math.log(1000000.0) / (HD // 2)))
    for s in range(STEPS):
        angle = (position + float(s)) * inverse
        cs[s] = jnp.cos(angle)
        sn[s] = jnp.sin(angle) * sign

    def mask(b, carry):
        rows = pl.ds(mult(b * 128, 128), 128)
        i = lax.broadcasted_iota(jnp.int32, (128, 1), 0) + b * 128
        r = i >> 4
        step = (i & 7) >> 1
        row_lane = lax.broadcasted_iota(jnp.int32, (1, ROWS), 1)
        limit = jnp.sum(jnp.where(row_lane == r + c * HALF, lengths, 0.0), axis=1, keepdims=True)
        place = lax.broadcasted_iota(jnp.int32, (1, CTX), 1).astype(F32)
        bias[rows, :] = jnp.where(place < limit, 0.0, -jnp.inf)
        n = lax.broadcasted_iota(jnp.int32, (1, 64), 1)
        usable = ((n & 15) == (r & 15)) & ((n >> 4) <= step)
        bias_f[rows, :] = jnp.where(usable, 0.0, -jnp.inf)
        return carry

    lax.fori_loop(0, 4, mask, 0)

    def project(i, carry):
        ks = pl.ds(mult(i * CHUNK, CHUNK), CHUNK)
        load_x(i).wait()
        load_wq(i).wait()
        load_wkv(i).wait()
        g = gain[:, ks]
        for s in range(STEPS):
            xs = xv[s, :, :, :, ks].reshape(ROWS, CHUNK).astype(F32)
            ybf[s] = (xs * g).astype(BF)
            xx = xs * xs
            total = xx[:, 0:128]
            for j in range(1, CHUNK // 128):
                total = total + xx[:, j * 128:(j + 1) * 128]
            sq[s] += total
        acc[...] += jnp.dot(
            ybf[...].reshape(STEPS * ROWS, CHUNK), w[ks, :], preferred_element_type=F32
        )
        return carry

    lax.fori_loop(0, 2, project, 0)

    best = dist[0] * 8
    for i in range(1, 8):
        best = jnp.minimum(best, dist[i] * 8 + i)
    chosen = lax.rem(best, 8)

    def order(t, carry):
        ordr[t] = hold[chosen, smap[t]]
        return carry

    pltpu.make_async_copy(hold, hold, ld.at[6]).wait()
    lax.fori_loop(0, 16, order, 0)

    pl.semaphore_wait(barrier, len(greet))

    def rows_of(xl_, xh_, y_, z_, c_):
        return pl.ds(mult(((xl_ * 4 + z_) * 16 + xh_ * 8 + y_ * 2 + c_) * 64, 64), 64)

    def to_ranks(source, rows, order_):
        groups = {}
        for k in order_:
            yk = ring(y, k)
            groups[k] = flag()
            for flip in (0, 1):
                if k or flip:
                    ck = (c, 1 - c)[flip]
                    send(source.at[yk * 2 + ck], nw.at[rows], dev(xl, xh, yk, z, ck), groups[k])
        return groups

    mine = rows_of(xl, xh, y, z, c)
    own_copies = to_ranks(ordr.at[pl.ds(mult(xh * 8, 8), 8)], mine, (0, 1, 3, 2))
    cross_copies = {}
    for k in (2, 1, 3, 0):
        cross_copies[k] = send(
            ordr.at[pl.ds((1 - xh) * 8 + ring(y, k) * 2, 2)],
            w1r.at[pl.ds(ring(y, k) * 2, 2)],
            cross,
        )
    nw[mine] = ordr[xh * 8 + y * 2 + c]
    wo_copy = send(wo_hbm.at[:, sib_cols], wo.at[my_wo], sibling)

    lax.fori_loop(2, 6, project, 0)

    def pair_of(xl_, xh_, k):
        return pl.ds(mult(((xl_ * 4 + z) * 16 + xh_ * 8 + ring(y, -k) * 2) * 64, 128), 128)

    slabs = {"0a": (xl, xh), "0b": (1 - xl, 1 - xh), "1a": (1 - xl, xh), "1b": (xl, 1 - xh)}
    z_groups = {name: (flag(), flag()) for name in slabs}
    last_z = flag()
    near_copies = {"a": {}, "b": {}}

    def around(name, k):
        ref = nw.at[pair_of(*slabs[name], k)]
        send(ref, ref, z_up, z_groups[name][0])
        send(ref, ref, z_down, z_groups[name][1])
        if name[0] == "0":
            near_copies[name[1]][k] = send(ref, ref, near)

    def onward(name):
        xl_, xh_ = slabs[name]
        arrived(z_groups[name][0])
        low = nw.at[pl.ds(mult(((xl_ * 4 + ring(z, -1)) * 16 + xh_ * 8) * 64, 256), 256)]
        send(low, low, z_up, last_z)
        arrived(z_groups[name][1])
        high = nw.at[pl.ds(mult(((xl_ * 4 + ring(z, 1)) * 16 + xh_ * 8) * 64 + 256, 256), 256)]
        send(high, high, z_down, last_z)

    theirs = rows_of(1 - xl, 1 - xh, y, z, c)
    theirs_copies = {}

    def serve_theirs(k):
        arrived(cross_copies[k])
        if k == 0:
            nw[theirs] = w1r[y * 2 + c]
        theirs_copies.update(to_ranks(w1r, theirs, (k,)))

    def first_around(k):
        arrived(own_copies[k])
        around("0a", k)

    def second_around(k):
        arrived(theirs_copies[k])
        around("0b", k)

    def near_around(part_, k):
        arrived(near_copies[part_][k])
        around("1" + part_, k)

    first_around(0)
    lax.fori_loop(6, NCHUNK, project, 0)

    def turn(v, s):
        return v * cs[s] + pltpu.roll(v, HD // 2, 1) * sn[s]

    for s in range(STEPS):
        scale = lax.rsqrt(jnp.sum(sq[s], axis=1, keepdims=True) * (1.0 / WIDTH) + 1e-06)
        block = pl.ds(s * ROWS, ROWS)
        for h in range(2):
            cols = slice(h * HD, (h + 1) * HD)
            qs[s, :, cols] = turn(acc[block, cols] * scale, s).astype(BF)
        if s == STEPS - 1:
            sib_half = pl.ds(mult((1 - c) * HALF, HALF), HALF)
            q_copy = send(qs.at[:, sib_half, :], qr, sibling)
    for s in range(STEPS):
        scale = lax.rsqrt(jnp.sum(sq[s], axis=1, keepdims=True) * (1.0 / WIDTH) + 1e-06)
        block = pl.ds(s * ROWS, ROWS)
        kn[s] = turn(acc[block, 256:384] * scale, s).astype(BF)
        vn[s] = (acc[block, 384:512] * scale).astype(BF)

    for s in range(STEPS):
        for h in range(2):
            qf[pl.ds(s * 2 + h, HALF, stride=16), :] = qs[s, my_half, h * HD:(h + 1) * HD].astype(
                F32
            )

    factor = 1.0 / math.sqrt(HD)

    def attend(b):
        block = pl.ds(b * 256, 256)
        sub = pl.ds(mult(c * HALF + b * 16, 16), 16)

        def score(i, carry):
            rows = pl.ds(mult(b * 256 + i * 16, 16), 16)
            mine_ = pl.ds(mult(i * 16, 16), 16)
            bias_here = bias[rows, :]
            got = lax.dot_general(
                qf[rows, :].astype(BF), kv[b * 16 + i, :, 0:HD], (((1,), (1,)), ((), ())),
                preferred_element_type=F32,
            )
            bias[rows, :] = got * factor + bias_here
            return carry

        lax.fori_loop(0, 16, score, 0, unroll=8)
        keys = kn[:, sub, :].reshape(STEPS * 16, HD)
        for part_of in range(2):
            rows = pl.ds(b * 256 + part_of * 128, 128)
            fresh = lax.dot_general(
                qf[rows, :].astype(BF), keys, (((1,), (1,)), ((), ())), preferred_element_type=F32
            ) * factor + bias_f[rows, :]
            cached = bias[rows, :]
            top = jnp.maximum(
                jnp.max(cached, axis=1, keepdims=True), jnp.max(fresh, axis=1, keepdims=True)
            )
            ce = jnp.exp(cached - top)
            fe = jnp.exp(fresh - top)
            total = jnp.sum(ce, axis=1, keepdims=True) + jnp.sum(fe, axis=1, keepdims=True)
            share = 1.0 / total
            pw[rows, :] = (ce * share).astype(BF)
            pf[rows, :] = (fe * share).astype(BF)
        values = vn[:, sub, :].reshape(STEPS * 16, HD)
        mix[block, :] = jnp.dot(pf[block, :], values, preferred_element_type=F32)

        def weigh(i, carry):
            rows = pl.ds(mult(b * 256 + i * 16, 16), 16)
            mix[rows, :] += jnp.dot(
                pw[rows, :], kv[b * 16 + i, :, HD:2 * HD], preferred_element_type=F32
            )
            return carry

        lax.fori_loop(0, 16, weigh, 0, unroll=8)
        for source in range(2):
            for s in range(STEPS):
                for h in range(2):
                    base = (c if source == 0 else 1 - c) * 256 + h * HD
                    att[b, s, c, :, pl.ds(mult(base, HD), HD)] = mix[
                        pl.ds(b * 256 + source * 8 + s * 2 + h, 16, stride=16), :
                    ].astype(BF)
        return send(att.at[b, :, c], att.at[b, :, c], sibling)

    def block_cols(yk, side):
        return pl.ds(mult(yk * 1024 + side * 512, 512), 512)

    def term(b, yk, side):
        cols = block_cols(yk, side)
        part[b, :, cols] = jnp.dot(
            att[b].reshape(128, 512), wo[:, cols], preferred_element_type=F32
        ).astype(BF)

    up, down, far = ring(y, 1), ring(y, -1), ring(y, 2)
    to_up, to_down, to_far = same_core(1), same_core(-1), same_core(2)
    o, n = 1 - xh, xh


    tasks = {}
    for k in range(4):
        tasks[f"W.s{k}"] = functools.partial(serve_theirs, k)
        tasks[f"W.q{k}"] = functools.partial(second_around, k)
        tasks[f"W.a{k}"] = functools.partial(near_around, "a", k)
        tasks[f"W.b{k}"] = functools.partial(near_around, "b", k)
    for name in slabs:
        tasks["W.o" + name] = functools.partial(onward, name)

    att_copies = {}

    def attend_to(b):
        if b == 0:
            arrived(q_copy)
            for s in range(STEPS):
                for h in range(2):
                    qf[pl.ds(8 + s * 2 + h, HALF, stride=16), :] = qr[
                        s, :, h * HD:(h + 1) * HD
                    ].astype(F32)
            load_kv.wait()
        att_copies[b] = attend(b)

    for b in range(2):
        tasks[f"attend{b}"] = functools.partial(attend_to, b)
    for k in (1, 2, 3):
        tasks[f"W.f{k}"] = functools.partial(first_around, k)
    made, ready = set(), set()

    def need(b, *blocks):
        if not ready:
            load_wo.wait()
            arrived(wo_copy)
        if b not in ready:
            ready.add(b)
            arrived(att_copies[b])
        for name, yk, side in blocks:
            if (b, name) not in made:
                made.add((b, name))
                term(b, yk, side)

    block_of = {
        "fo": (far, o), "fn": (far, n), "uo": (up, o), "un": (up, n),
        "do": (down, o), "dn": (down, n), "o": (y, o), "n": (y, n),
    }
    to_sibling = flag()

    def chunk_at(c_, y_, xh_, off=0, size=512):
        return pl.ds(mult(c_ * COLS + y_ * 1024 + xh_ * 512 + off, 128), size)

    own = chunk_at(c, y, xh)
    other = chunk_at(c, y, 1 - xh)

    def add_group(g, b, step, steps, kind):
        rows = steps * 32
        span = pl.ds(step * 32, rows)
        f = {}

        def slot(ref, *index):
            return ref.at[(g,) + index + (pl.ds(0, rows),)]

        def mine_of(name):
            need(b, (name,) + block_of[name])
            return part.at[b, span, block_cols(*block_of[name])]

        def wide(ref):
            return ref[...].astype(F32)

        def out_at(cols):
            return out.at[pl.ds(step, steps), :, b, :, cols]

        def give(cols, where, group=None):
            return send(out_at(cols), out_at(cols), where, group, 1)

        def share(cols):
            send(out_at(cols), out_at(cols), sibling, to_sibling, 2)

        def finish(total, cols):
            ref = xv.at[pl.ds(step, steps), :, b, :, cols]
            out_at(cols)[...] = (wide(ref) + total.reshape(steps, 2, 16, 512)).astype(BF)

        def add(name, run):
            tasks[f"g{g}.{name}"] = run

        def relay():
            f["ru"] = send(mine_of("fo"), slot(rel_up), to_up, lane=3)
            f["rd"] = send(mine_of("fn"), slot(rel_dn), to_down, lane=3)

        def direct():
            f["o"], f["n"] = flag(), flag()
            send(mine_of("do"), slot(dir_o), to_down, f["o"], 3)
            send(mine_of("un"), slot(dir_n), to_up, f["n"], 3)

        def sum_up():
            first = wide(mine_of("uo"))
            arrived(f["ru"])
            slot(s_up)[...] = (first + wide(slot(rel_up))).astype(BF)
            send(slot(s_up), slot(sum_o), to_up, f["o"], 3)

        def sum_down():
            first = wide(mine_of("dn"))
            arrived(f["rd"])
            slot(s_dn)[...] = (first + wide(slot(rel_dn))).astype(BF)
            send(slot(s_dn), slot(sum_n), to_down, f["n"], 3)

        def own_sum(q, more, added):
            first = wide(mine_of(q))
            arrived(f[q])
            slot(sa, "no".index(q))[...] = (first + wide(more) + wide(added)).astype(BF)
            ref = slot(sa, "no".index(q))
            f["x" + q] = send(ref, slot(rax, "on".index(q)), across, lane=3)

        def finish_a(q, cols):
            arrived(f["x" + ("o" if q == "n" else "n")])
            i = "no".index(q)
            finish(wide(slot(sa, i)) + wide(slot(rax, i)), cols)
            f["gu" + q] = give(cols, to_up)
            f["gd" + q] = give(cols, to_down)
            share(cols)

        def half_up(q, side):
            arrived(f["gu" + q])
            if "h" + q not in f:
                f["h" + q] = flag()
            give(chunk_at(c, down, side, 0, 256), to_up, f["h" + q])
            share(chunk_at(c, down, side))

        def half_down(q, side):
            arrived(f["gd" + q])
            if "h" + q not in f:
                f["h" + q] = flag()
            give(chunk_at(c, up, side, 256, 256), to_down, f["h" + q])
            share(chunk_at(c, up, side))

        def last_far(q, side):
            arrived(f["h" + q])
            share(chunk_at(c, far, side))

        to = {"f": (far, to_far), "u": (up, to_up), "d": (down, to_down)}

        def start(k):
            cols = k + "o" if k in to else "o"
            f["x" + k] = send(mine_of(cols), slot(rbx, "fudo".index(k)), across, lane=3)

        def pass_on(k):
            first = wide(mine_of(k + "n"))
            arrived(f["x" + k])
            i = "fud".index(k)
            if "y" not in f:
                f["y"] = flag()
            if kind == "Br" and k == "f":
                slot(sb, i)[...] = (first + wide(slot(rbx, i))).astype(BF)
                f["hu"] = send(
                    slot(sb, i).at[:, pl.ds(0, 256)], slot(rbh, 0), to_up, lane=3
                )
                f["hd"] = send(
                    slot(sb, i).at[:, pl.ds(256, 256)], slot(rbh, 1), to_down, lane=3
                )
                return
            total = first + wide(slot(rbx, i))
            if kind == "Br":
                arrived(f["h" + k])
                if k == "u":
                    more = jnp.concatenate(
                        [total[:, :256] + wide(slot(rbh, 0)), total[:, 256:]], axis=1
                    )
                else:
                    more = jnp.concatenate(
                        [total[:, :256], total[:, 256:] + wide(slot(rbh, 1))], axis=1
                    )
                total = more
            slot(sb, i)[...] = total.astype(BF)
            send(slot(sb, i), slot(rb, i), to[k][1], f["y"], 3)

        def pass_own():
            first = wide(mine_of("n"))
            arrived(f["xo"])
            slot(keep)[...] = first + wide(slot(rbx, 3))

        def finish_b():
            arrived(f["y"])
            total = slot(keep)[...] + wide(slot(rb, 1)) + wide(slot(rb, 2))
            if kind == "B":
                total = total + wide(slot(rb, 0))
            finish(total, own)
            if kind == "B":
                f["gf"] = give(own, to_far)
            f["gu"] = give(own, to_up)
            f["gd"] = give(own, to_down)
            f["gx"] = give(own, across)
            share(own)

        source = {"f": far, "u": down, "d": up}

        def to_across(k):
            arrived(f["g" + k])
            if kind == "Br" and k != "f":
                if "gf" not in f:
                    f["gf"] = flag()
                if k == "u":
                    give(chunk_at(c, down, xh, 0, 256), to_up, f["gf"])
                else:
                    give(chunk_at(c, up, xh, 256, 256), to_down, f["gf"])
            f["z" + k] = give(chunk_at(c, source[k], xh), across)
            share(chunk_at(c, source[k], xh))

        def last_across(k):
            arrived(f["z" + k])
            share(chunk_at(c, source[k], 1 - xh))

        def last_own():
            arrived(f["gx"])
            share(other)

        if kind == "A":
            add("relay", relay)
            add("direct", direct)
            add("sumu", sum_up)
            add("sumd", sum_down)
            add("o", functools.partial(own_sum, "o", slot(dir_o), slot(sum_o)))
            add("n", functools.partial(own_sum, "n", slot(dir_n), slot(sum_n)))
            for q, side, cols in (("n", xh, own), ("o", 1 - xh, other)):
                add("fin" + q, functools.partial(finish_a, q, cols))
                add(f"r{q}u", functools.partial(half_up, q, side))
                add(f"r{q}d", functools.partial(half_down, q, side))
                add("l" + q, functools.partial(last_far, q, side))
        else:
            for k in "fudo":
                add("b" + k, functools.partial(start, k))
            for k in "fud":
                add("p" + k, functools.partial(pass_on, k))
                add("a" + k, functools.partial(to_across, k))
                add("l" + k, functools.partial(last_across, k))
            add("po", pass_own)
            add("fin", finish_b)
            add("lx", last_own)

    for g, spec in enumerate(GROUPS):
        add_group(g, *spec)
    assert sorted(ORDER) == sorted(tasks)
    for name in ORDER:
        tasks[name]()

    assert len(used) <= NCOPY
    for i in list(pending):
        arrived(i)
    for lane_, amount in enumerate(sent):
        wait_kib(ssem.at[lane_], amount)


def store(out_ref, nw_ref, out_hbm, nw_hbm, sem):
    copies = [
        pltpu.make_async_copy(out_ref, out_hbm, sem.at[0]),
        pltpu.make_async_copy(nw_ref, nw_hbm, sem.at[1]),
    ]
    for cp in copies:
        cp.start()
    for cp in copies:
        cp.wait()


def on_device(
    inputs, norm_gain, w_query, w_kv, w_out, kv_cache, kv_lengths, reuse_dist, shard_map,
    holder_weights,
):
    hbm = pl.BlockSpec(memory_space=pltpu.HBM)
    vmem = pl.BlockSpec(memory_space=pltpu.VMEM)
    dma = pltpu.SemaphoreType.DMA
    block = (len(GROUPS), 64, 512)
    outputs, next_weights = pl.pallas_call(
        kernel,
        out_shape=(
            pltpu.VMEM((STEPS, 2, 2, 16, WIDTH), BF),
            pltpu.VMEM((WIDTH, 256), BF),
        ),
        in_specs=[hbm] * 10,
        out_specs=(vmem, vmem),
        scratch_shapes=[
            pltpu.VMEM((1, WIDTH), F32),
            pltpu.VMEM((1, ROWS), jnp.int32),
            pltpu.SMEM((8,), jnp.int32),
            pltpu.SMEM((16,), jnp.int32),
            pltpu.VMEM((STEPS, 2, 2, 16, WIDTH), BF),
            pltpu.VMEM((WIDTH, 512), BF),
            pltpu.VMEM((512, COLS), BF),
            pltpu.VMEM((HALF, CTX, 2 * HD), BF),
            pltpu.VMEM((8, 16, 64, 256), BF),
            pltpu.VMEM((16, 64, 256), BF),
            pltpu.VMEM((8, 64, 256), BF),
            pltpu.VMEM((STEPS * ROWS, 512), F32),
            pltpu.VMEM((STEPS, ROWS, 128), F32),
            pltpu.VMEM((STEPS, ROWS, CHUNK), BF),
            pltpu.VMEM((STEPS, ROWS, HD), F32),
            pltpu.VMEM((STEPS, ROWS, HD), F32),
            pltpu.VMEM((STEPS, ROWS, 256), BF),
            pltpu.VMEM((STEPS, HALF, 256), BF),
            pltpu.VMEM((STEPS, ROWS, HD), BF),
            pltpu.VMEM((STEPS, ROWS, HD), BF),
            pltpu.VMEM((512, HD), F32),
            pltpu.VMEM((512, CTX), F32),
            pltpu.VMEM((512, 64), F32),
            pltpu.VMEM((512, CTX), BF),
            pltpu.VMEM((512, 64), BF),
            pltpu.VMEM((512, HD), F32),
            pltpu.VMEM((2, STEPS, 2, 16, 512), BF),
            pltpu.VMEM((2, 128, COLS), BF),
            pltpu.VMEM((len(GROUPS), 4, 64, 512), BF),
            pltpu.VMEM((len(GROUPS), 3, 64, 512), BF),
            pltpu.VMEM((len(GROUPS), 3, 64, 512), BF),
            pltpu.VMEM(block, BF),
            pltpu.VMEM(block, BF),
            pltpu.VMEM(block, BF),
            pltpu.VMEM(block, BF),
            pltpu.VMEM(block, BF),
            pltpu.VMEM(block, BF),
            pltpu.VMEM(block, BF),
            pltpu.VMEM(block, BF),
            pltpu.VMEM((len(GROUPS), 2, 64, 512), BF),
            pltpu.VMEM((len(GROUPS), 2, 64, 512), BF),
            pltpu.VMEM((len(GROUPS), 2, 64, 256), BF),
            pltpu.VMEM(block, F32),
            dma((7,)),
            dma((NCHUNK, 3)),
            dma((4,)),
            dma((NCOPY,)),
        ],
        compiler_params=pltpu.CompilerParams(
            collective_id=0, has_side_effects=True, vmem_limit_bytes=48 * 1024 * 1024
        ),
    )(
        inputs.reshape(STEPS, 2, 2, 16, WIDTH), norm_gain.reshape(1, WIDTH), w_query, w_kv, w_out,
        kv_cache, kv_lengths.reshape(1, ROWS), reuse_dist, shard_map, holder_weights,
    )
    outputs, next_weights = pl.pallas_call(
        store,
        out_shape=(
            pltpu.HBM((STEPS, 2, 2, 16, WIDTH), BF),
            pltpu.HBM((WIDTH, 256), BF),
        ),
        in_specs=[vmem, vmem],
        out_specs=(hbm, hbm),
        scratch_shapes=[dma((2,))],
        compiler_params=pltpu.CompilerParams(vmem_limit_bytes=4 * 1024 * 1024),
    )(
        pltpu.with_memory_space_constraint(outputs, pltpu.VMEM),
        pltpu.with_memory_space_constraint(next_weights, pltpu.VMEM),
    )
    return outputs.reshape(STEPS, ROWS, WIDTH), next_weights


def solution(mesh):
    in_specs = (
        P(None, "dp", None),
        P(),
        P(None, "tensor"),
        P(None, "tensor"),
        P("tensor", None),
        P("dp", "tensor", None, None),
        P("dp"),
        P(),
        P(),
        P(None, ("dp", "tensor"), None),
    )
    out_specs = (P(None, "dp", None), P(None, "tensor"))
    return jax.shard_map(
        on_device, mesh=mesh, in_specs=in_specs, out_specs=out_specs, check_vma=False
    )
```
